128 devices in a mesh: ta: 8 (over y, core), xyz: 16 (over x, z).
Axes of the slice: x: 4, y: 4, z: 4, core: 2. Of those that a mesh axis runs over, the one named last changes fastest.
Arguments:
- source: float32 [4, 2, 32, 128, 4, 128], P(None, None, 'ta', 'xyz'), may hold values from -6 to 6
- mass: float32 [32, 128, 4, 128], P('ta', 'xyz'), may hold values from 0.2 to 4
- links: int32 [4, 32, 128, 4, 128], P(None, 'ta', 'xyz'), may hold values from 0 to 1
- near_null: bfloat16 [24, 4, 32, 128, 4, 128], P(None, None, 'ta', 'xyz'), may hold values from -0.1875 to 0.1875
- coarse_op: bfloat16 [9, 24, 24, 8, 32, 1, 32], P(None, None, None, 'ta', 'xyz'), may hold values from -0.09 to 1.1
- plan: int32 [8], replicated, may hold values from 0 to 1
Outputs:
- solution: float32 [4, 2, 32, 128, 4, 128], P(None, None, 'ta', 'xyz')
- residual: float32 [4, 2, 32, 128, 4, 128], P(None, None, 'ta', 'xyz')
The draws below stay inside these ranges and needn't reach their ends.
All inputs are finite; a program needn't handle non-finite values.
Results may differ from the reference program's by a relative error of at most 0.011.
Values may be sent and summed in bfloat16 or wider, within the bound.
No kernel may reach another device: no remote copies, remote signals or barrier semaphores. Data moves between devices by JAX's collectives and lax.ppermute only.
A program may use at most 192 MiB of HBM per device.

```python
import jax
import jax.numpy as jnp
import numpy as np
from jax import lax

SPIN = 4
RHS = 2
NVEC = 24
AGG = 4
NY = 4
NZ = 128
SWEEPS = 8
KC = 6
TT = 32
XX = 128


def draw_coarse_op(key, part):
    key = jax.random.fold_in(key, 7)
    shape = (9, NVEC, NVEC, TT // AGG, XX // AGG, NY // AGG, NZ // AGG)
    noise = jnp.clip(0.05 * jax.random.normal(key, shape, jnp.float32), -0.09, 0.09)
    block_zero = (jnp.arange(9) == 0).astype(jnp.float32)[:, None, None, None, None, None, None]
    ident = jnp.eye(NVEC, dtype=jnp.float32)[None, :, :, None, None, None, None]
    return (noise + block_zero * ident).astype(jnp.bfloat16)


def place_ends(values, own_key, low, top_value):
    dims = values.shape
    place = [jax.random.randint(jax.random.fold_in(own_key, axis), (), 0, dims[axis]) for axis in range(len(dims))]
    values = values.at[tuple(place)].set(low)
    longest = dims.index(max(dims))
    place[longest] = (place[longest] + 1) % dims[longest]
    return values.at[tuple(place)].set(top_value)


def steps_of(key, extent, cuts, least, top_value):
    def one(position, blocks):
        steps = jax.random.uniform(jax.random.fold_in(jax.random.fold_in(key, 6), position), (blocks,), jnp.float32, least / len(cuts), top_value / len(cuts))
        return jnp.repeat(jnp.exp(steps), extent[position] // blocks).reshape((-1,) + (1,) * (len(extent) - position - 1))

    factor_of = one(*cuts[0])
    for cut in cuts[1:]:
        factor_of = factor_of * one(*cut)
    return factor_of


def scatter_about(stream_key, extent, scale, limit, cuts=(), held_as=jnp.bfloat16):
    drawn = scale * jax.random.normal(stream_key, extent, jnp.float32)
    if cuts:
        drawn = drawn * steps_of(stream_key, extent, cuts, -0.22, 0.18)
    return jnp.clip(drawn, -limit, limit).astype(held_as)


def setup_inputs(seed: int = 0) -> dict:
    streams_of = jax.random.split(jax.random.key(seed), 7)
    return {
        "source": scatter_about(streams_of[0], (SPIN, RHS, TT, XX, NY, NZ), 1.0, 6.0, ((2, 8), (3, 16)), jnp.float32),
        "mass": jnp.clip(0.2 + 3.8 * jax.random.uniform(streams_of[1], (TT, XX, NY, NZ), jnp.float32) ** steps_of(streams_of[1], (TT, XX, NY, NZ), ((0, 8), (1, 16)), -0.2, 0.2), 0.2, 4.0),
        "links": place_ends(jax.random.randint(streams_of[2], (4, TT, XX, NY, NZ), 0, 2), jax.random.fold_in(streams_of[2], 1), 0, 1).astype(jnp.int32),
        "near_null": scatter_about(streams_of[3], (NVEC, SPIN, TT, XX, NY, NZ), 1024 ** -0.5, 0.1875, ((2, 8), (3, 16))),
        "coarse_op": draw_coarse_op(jax.random.fold_in(streams_of[6], 71), 0),
        "plan": place_ends(jax.random.randint(streams_of[5], (SWEEPS,), 0, 2), jax.random.fold_in(streams_of[5], 1), 0, 1).astype(jnp.int32),
    }


def gamma_table():
    sigma_x = np.array([[0.0, 1.0], [1.0, 0.0]], np.float32)
    sigma_z = np.array([[1.0, 0.0], [0.0, -1.0]], np.float32)
    rotate = np.array([[0.0, -1.0], [1.0, 0.0]], np.float32)
    ident = np.eye(2, dtype=np.float32)
    return np.stack([np.kron(sigma_x, ident), np.kron(sigma_z, sigma_x), np.kron(sigma_z, sigma_z), -np.kron(rotate, rotate)])


def spin_turn(direction, values):
    table = gamma_table()[direction]
    pieces = []
    for row in range(4):
        column = int(np.argmax(np.abs(table[row])))
        factor = float(table[row, column])
        pieces.append(factor * values[column])
    return jnp.stack(pieces, 0)


def fine_apply(padded, signs, diag):
    centre = padded[:, :, 1:-1, 1:-1]
    pairs = ((padded[:, :, 2:, 1:-1], padded[:, :, :-2, 1:-1]),
             (padded[:, :, 1:-1, 2:], padded[:, :, 1:-1, :-2]),
             (jnp.roll(centre, -1, 4), jnp.roll(centre, 1, 4)),
             (jnp.roll(centre, -1, 5), jnp.roll(centre, 1, 5)))
    total = diag[None, None] * centre
    for direction in range(4):
        ahead, behind = pairs[direction]
        turned = spin_turn(direction, ahead - behind)
        total = total - signs[direction][None, None] * (0.5 * (ahead + behind) - 0.5 * turned)
    return total


def blocked(array):
    lead = array.shape[:2]
    inner = []
    for length in array.shape[2:]:
        inner.append(length // AGG)
        inner.append(AGG)
    return array.reshape(lead + tuple(inner))


def restrict(vectors, field):
    return jnp.einsum("ksAiBjClEm,snAiBjClEm->knABCE", blocked(vectors), blocked(field), preferred_element_type=jnp.float32)


def prolong(vectors, coarse, shape):
    fine = jnp.einsum("ksAiBjClEm,knABCE->snAiBjClEm", blocked(vectors), coarse, preferred_element_type=jnp.float32)
    return fine.reshape(shape)


def coarse_apply(padded, operator):
    centre = padded[:, :, 1:-1, 1:-1]
    beside_all = [centre, padded[:, :, 2:, 1:-1], padded[:, :, :-2, 1:-1], padded[:, :, 1:-1, 2:], padded[:, :, 1:-1, :-2],
              jnp.roll(centre, -1, 4), jnp.roll(centre, 1, 4), jnp.roll(centre, -1, 5), jnp.roll(centre, 1, 5)]
    total = jnp.einsum("kjABCE,jnABCE->knABCE", operator[0], beside_all[0], preferred_element_type=jnp.float32)
    for index in range(1, 9):
        total = total + jnp.einsum("kjABCE,jnABCE->knABCE", operator[index], beside_all[index], preferred_element_type=jnp.float32)
    return total


def wrap_both(field):
    return jnp.pad(field, ((0, 0), (0, 0), (1, 1), (1, 1), (0, 0), (0, 0)), mode="wrap")


def reference(source, mass, links, near_null, coarse_op, plan):
    signs = (1 - 2 * links).astype(jnp.float32)
    diag = 4.0 + mass
    shape4 = mass.shape
    parity = (lax.broadcasted_iota(jnp.int32, shape4, 0) // AGG + lax.broadcasted_iota(jnp.int32, shape4, 1) // AGG
              + lax.broadcasted_iota(jnp.int32, shape4, 2) // AGG + lax.broadcasted_iota(jnp.int32, shape4, 3) // AGG) % 2

    def residual_of(field):
        return source - fine_apply(wrap_both(field), signs, diag)

    def update(field, resid, colour):
        chosen = jnp.where(parity == colour, 1.0, 0.0).astype(jnp.float32)
        return field + chosen[None, None] * resid / diag[None, None]

    solution = jnp.zeros(source.shape, jnp.float32)
    half = SWEEPS // 2
    for sweep in range(half):
        solution = update(solution, residual_of(solution), plan[sweep])
    fine_residual = residual_of(solution).astype(jnp.bfloat16)
    coarse_rhs = restrict(near_null, fine_residual)
    estimate = coarse_rhs
    for turn in range(1, KC):
        rounded = estimate.astype(jnp.bfloat16)
        estimate = estimate + (coarse_rhs - coarse_apply(wrap_both(rounded), coarse_op))
    solution = solution + prolong(near_null, estimate.astype(jnp.bfloat16), source.shape)
    for sweep in range(half, SWEEPS):
        solution = update(solution, residual_of(solution), plan[sweep])
    return solution, residual_of(solution)
```

```python
import jax
import jax.numpy as jnp
from jax import lax
from jax.experimental import pallas as pl
from jax.experimental.pallas import tpu as pltpu
from jax.sharding import PartitionSpec as P

LT, ROWS, LANES = 4, 32, 128
NVEC, RHS, KC, SWEEPS = 24, 2, 6, 8
ET, EROWS, PAD = 12, 80, 8
FIELDS = 13
F32, BF16, I32 = jnp.float32, jnp.bfloat16, jnp.int32
T_INDEX, X_INDEX = SWEEPS, SWEEPS + 1


def params(mebibytes):
    return pltpu.CompilerParams(vmem_limit_bytes=mebibytes * 1024 * 1024)


def shape(dims, dtype):
    return jax.ShapeDtypeStruct(dims, dtype)


VM = pl.BlockSpec(memory_space=pltpu.VMEM)
SM = pl.BlockSpec(memory_space=pltpu.SMEM)


def roll(values, shift, axis):
    return pltpu.roll(values, shift, axis)


def tile_iotas():
    row = lax.broadcasted_iota(I32, (8, LANES), 0)
    lane = lax.broadcasted_iota(I32, (8, LANES), 1)
    return row, lane


def x_pair(spins):
    ahead = (spins[0] - spins[1], spins[2] + spins[3])
    behind = (spins[0] + spins[1], spins[2] - spins[3])
    return [roll(value, 4, 0) for value in ahead + behind]


def hops(centre, before, after, ahead_t, behind_t, coefs, row):
    first = row < 4
    top = (row & 3) == 0
    bottom = (row & 3) == 3
    sign_t, sign_x, sign_y, sign_z = coefs
    p0, p1 = ahead_t[0] - ahead_t[2], ahead_t[1] - ahead_t[3]
    q0, q1 = behind_t[0] + behind_t[2], behind_t[1] + behind_t[3]
    along_t = (q0 + p0, q1 + p1, q0 - p0, q1 - p1)
    here = centre[1]
    u0, u2 = (jnp.where(first, here[i], after[i]) for i in (0, 1))
    w0, w2 = (jnp.where(first, before[i], here[i]) for i in (2, 3))
    along_x = (w0 + u0, w0 - u0, u2 + w2, u2 - w2)
    v = centre[0]

    def back(value):
        return jnp.where(top, roll(value, 5, 0), roll(value, 1, 0))

    def forth(value):
        return jnp.where(bottom, roll(value, 3, 0), roll(value, 7, 0))

    along_y = (back(v[0]), forth(v[1]), forth(v[2]), back(v[3]))
    f, g = roll(v[0] + v[3], LANES - 1, 1), roll(v[1] - v[2], LANES - 1, 1)
    h, k = roll(v[0] - v[3], 1, 1), roll(v[1] + v[2], 1, 1)
    along_z = (f + h, k + g, k - g, f - h)
    return [
        (sign_t * along_t[s] + sign_x * along_x[s]) + (sign_y * along_y[s] + sign_z * along_z[s])
        for s in range(4)
    ]


def visit(field, signs, slices, tiles, put, row):
    lows = slices[0::2]
    length = slices[1] - slices[0]

    def body(step, carry):
        t = step + lows[0] if len(lows) == 1 else jnp.where(step < length, step + lows[0], step - length + lows[1])

        def spins_at(time, tile, side):
            start = PAD + 8 * tile
            return [field[2 * s + side, time, start : start + 8, :] for s in range(4)]

        for side in range(RHS):
            spins = {}
            pairs = {}
            for tile in range(tiles[0] - 1, tiles[1] + 1):
                spins[tile] = spins_at(t, tile, side)
                pairs[tile] = x_pair(spins[tile])
            for tile in range(*tiles):
                start = PAD + 8 * tile
                coefs = [signs[m, t, start : start + 8, :] for m in range(4)]
                sums = hops(
                    (spins[tile], pairs[tile]),
                    pairs[tile - 1],
                    pairs[tile + 1],
                    spins_at(t + 1, tile, side),
                    spins_at(t - 1, tile, side),
                    coefs,
                    row,
                )
                put(t, tile, side, spins[tile], sums)
        return carry

    lax.fori_loop(0, length * len(lows), body, 0)


def chosen(scal, colour, t, tile, lane):
    block = scal[T_INDEX] + t // 4 + 1 + tile // 2 + 1
    return ((lane >> 2) & 1) == ((scal[colour] + block) & 1)


def half_sweep(scal, colour, target, field, source, signs, inverse, slices, tiles, row, lane):
    def put(t, tile, side, centre, sums):
        start = PAD + 8 * tile
        mask = chosen(scal, colour, t, tile, lane)
        scale = inverse[t, start : start + 8, :]
        for s in range(4):
            value = (source[2 * s + side, t, start : start + 8, :] + sums[s]) * scale
            target[2 * s + side, t, start : start + 8, :] = jnp.where(mask, value, centre[s])

    visit(field, signs, slices, tiles, put, row)


def three_sweeps(scal, colour, field_a, field_b, src, signs, inverse, row, lane):
    def sweep(number, target, field, slices, tiles):
        half_sweep(scal, colour + number, target, field, src, signs, inverse, slices, tiles, row, lane)

    sweep(0, field_b, field_a, (4, 8), (0, 8))
    sweep(0, field_b, field_a, (2, 4, 8, 10), (1, 7))
    sweep(0, field_b, field_a, (1, 2, 10, 11), (2, 6))
    sweep(1, field_a, field_b, (3, 9), (1, 7))
    sweep(1, field_a, field_b, (2, 3, 9, 10), (2, 6))
    sweep(2, field_b, field_a, (4, 8), (1, 7))
    sweep(2, field_b, field_a, (3, 4, 8, 9), (2, 6))


def places(scal):
    t_odd, x_odd = scal[T_INDEX] & 1, scal[X_INDEX] & 1
    return (t_odd, 1 - t_odd), (x_odd, 1 - x_odd)


def put_halos(scal, fields, ta, tb, xa, xb, ca, cb, put, add_low, first):
    t_before, x_before = places(scal)

    def x_start(before):
        return pl.multiple_of(PAD + 48 * (1 - before), 8)

    for data, before in ((ta, t_before[0]), (tb, t_before[1])):
        base = 8 * (1 - before)

        def t_slice(t, carry, data=data, base=base):
            for c in range(fields):
                put(c, base + t, slice(PAD + 16, PAD + 48), data[fields * t + c].astype(F32))
            return carry

        lax.fori_loop(0, LT, t_slice, 0)
        near = 8 - 5 * before
        for c in range(8):
            add_low(c, near, slice(PAD + 16, PAD + 48), data[4 * fields + c].astype(F32))
    for data, before in ((xa, x_before[0]), (xb, x_before[1])):
        start = x_start(before)

        def x_slice(t, carry, data=data, start=start):
            for c in range(fields):
                put(c, 4 + t, pl.ds(start, 16), data[fields * t + c].astype(F32))
            return carry

        lax.fori_loop(0, LT, x_slice, 0)
        where = pl.ds(pl.multiple_of(start + 8 * before, 8), 8)
        for c in range(8):
            low = data[4 * fields + c].astype(F32)
            for t in range(LT):
                pair = low[8 * (t // 2) : 8 * (t // 2) + 8]
                turned = roll(pair, 4, 0)
                top, bottom = (pair, turned) if t % 2 == 0 else (turned, pair)
                value = jnp.where(before == 0, jnp.where(first, top, 0.0), jnp.where(first, 0.0, bottom))
                add_low(c, 4 + t, where, value)
    for data, before in ((ca, t_before[0]), (cb, t_before[1])):
        near, step = 8 - 5 * before, 1 - 2 * before
        for c in range(fields):
            for half in range(2):
                start = x_start(x_before[half])
                put(c, near, pl.ds(start, 16), data[c, 16 * half : 16 * half + 16, :].astype(F32))
                value = data[fields + c, 16 * half : 16 * half + 16, :].astype(F32)
                where = pl.ds(pl.multiple_of(start + 8 * x_before[half], 8), 8)
                put(c, near + step, where, value[:8])
                put(c, near + 2 * step, where, value[8:])


def pack_shares(scal, fields, read, t_a, t_b, x_a, x_b, first):
    t_before, x_before = places(scal)

    def one_slice(t, carry):
        for c in range(fields):
            value = read(c, t).astype(BF16)
            t_a[fields * t + c] = value
            t_b[fields * t + c] = value
            x_a[fields * t + c] = jnp.where(x_before[0] == 0, value[16:], value[:16])
            x_b[fields * t + c] = jnp.where(x_before[1] == 0, value[16:], value[:16])
        return carry

    lax.fori_loop(0, LT, one_slice, 0)

    def low_part(value):
        return value - value.astype(BF16).astype(F32)

    for c in range(8):
        for out, before in ((t_a, t_before[0]), (t_b, t_before[1])):
            out[4 * fields + c] = low_part(read(c, 3 * (1 - before))).astype(BF16)
        ends = [(value[:8], value[24:]) for value in (low_part(read(c, t)) for t in range(LT))]
        lows, highs = [], []
        for t in (0, 2):
            lows.append(jnp.where(first, ends[t][0], roll(ends[t + 1][0], 4, 0)))
            highs.append(jnp.where(first, roll(ends[t][1], 4, 0), ends[t + 1][1]))
        low, high = jnp.concatenate(lows, 0), jnp.concatenate(highs, 0)
        for out, before in ((x_a, x_before[0]), (x_b, x_before[1])):
            out[4 * fields + c] = jnp.where(before == 0, high, low).astype(BF16)


def corner_kernel(scal, xa, xb, ca, cb):
    fields = ca.shape[0] // 2
    t_before, x_before = places(scal)
    for out, before in ((ca, t_before[0]), (cb, t_before[1])):
        near, step = 3 * (1 - before), 2 * before - 1

        def one_field(c, carry, out=out, near=near, step=step):
            for half, data in enumerate((xa, xb)):
                where = slice(16 * half, 16 * half + 16)
                out[c, where, :] = data[fields * near + c]
                pieces = []
                for depth in (1, 2):
                    value = data[fields * (near + depth * step) + c].astype(F32)
                    pieces.append(jnp.where(x_before[half] == 0, value[:8], value[8:]))
                out[fields + c, where, :] = jnp.concatenate(pieces, 0).astype(BF16)
            return carry

        lax.fori_loop(0, fields, one_field, 0)


def fill_inputs(scal, source, mass, links, halos, src, signs, inverse):
    own = slice(PAD + 16, PAD + 48)

    def own_slice(t, carry):
        for c in range(8):
            src[c, t + 4, own, :] = source[c, t]
        for m in range(4):
            scale = 2.0 if m == 2 else 1.0
            signs[m, t + 4, own, :] = scale * (0.5 - links[m, t].astype(F32))
        inverse[t + 4, own, :] = 1.0 / (4.0 + mass[t])
        return carry

    lax.fori_loop(0, LT, own_slice, 0)

    def put(c, t, rows, value):
        if c < 8:
            src[c, t, rows, :] = value
        elif c == 8:
            inverse[t, rows, :] = 1.0 / (4.0 + value)
        else:
            signs[c - 9, t, rows, :] = value

    def add_low(c, t, rows, value):
        src[c, t, rows, :] = src[c, t, rows, :] + value

    first = lax.broadcasted_iota(I32, (8, LANES), 0) < 4
    put_halos(scal, FIELDS, *halos, put, add_low, first)


def pack_kernel(scal, source, mass, links, t_a, t_b, x_a, x_b):
    def read(c, t):
        if c < 8:
            return source[c, t]
        if c == 8:
            return mass[t]
        return (1.0 if c == 11 else 0.5) * (1 - 2 * links[c - 9, t]).astype(F32)

    first = lax.broadcasted_iota(I32, (8, LANES), 0) < 4
    pack_shares(scal, FIELDS, read, t_a, t_b, x_a, x_b, first)


def relayout_kernel(operator, result):
    def group(kk, carry):
        def block(b, q):
            return operator[b, 4 * kk + q].astype(F32)

        for place, kinds in enumerate(((0, 5, 6), (1,), (2,), (3,), (4,), (7,), (8,))):
            pieces = []
            for q in range(4):
                piece = block(kinds[0], q)
                for b in kinds[1:]:
                    piece = piece + block(b, q)
                pieces.append(piece)
            result[place, kk] = jnp.concatenate(pieces, axis=-1)
        return carry

    lax.fori_loop(0, 6, group, 0)


def exact_sum(matrix, values, left):
    high = values.astype(BF16)
    low = (values - high.astype(F32)).astype(BF16)

    def one(part):
        pair = (matrix, part) if left else (part, matrix)
        return jnp.dot(*pair, preferred_element_type=F32)

    return one(high) + one(low)


def pre_kernel(
    scal, source, mass, links, ta, tb, xa, xb, ca, cb, near_null,
    out_solution, out_rhs, out_rounded,
    src, signs, inverse, field_a, field_b, resid, sums,
):
    row, lane = tile_iotas()
    fill_inputs(scal, source, mass, links, (ta, tb, xa, xb, ca, cb), src, signs, inverse)

    def first_sweep(t, carry):
        for tile in range(8):
            start = PAD + 8 * tile
            mask = chosen(scal, 0, t, tile, lane)
            scale = jnp.where(mask, inverse[t, start : start + 8, :], 0.0)
            for c in range(8):
                field_a[c, t, start : start + 8, :] = src[c, t, start : start + 8, :] * scale
        return carry

    lax.fori_loop(0, ET, first_sweep, 0)
    three_sweeps(scal, 1, field_a, field_b, src, signs, inverse, row, lane)

    def put(t, tile, side, centre, hop):
        start = PAD + 8 * tile
        inner = 8 * (tile - 2)
        diag = 4.0 + mass[t - 4, inner : inner + 8, :]
        for s in range(4):
            c = 2 * s + side
            value = (src[c, t, start : start + 8, :] - diag * centre[s]) + hop[s]
            resid[c, t - 4, inner : inner + 8, :] = value.astype(BF16).astype(F32)
            out_solution[c, t - 4, inner : inner + 8, :] = centre[s]

    visit(field_b, signs, (4, 8), (2, 6), put, row)

    group = 4

    def vectors(step, carry):
        totals = {}
        for s in range(4):
            for t in range(LT):
                for block in range(2):
                    low, mid, high = 16 * block, 16 * block + 8, 16 * block + 16
                    halves = [
                        (resid[2 * s + n, t, low:mid, :], resid[2 * s + n, t, mid:high, :]) for n in range(RHS)
                    ]
                    for i in range(group):
                        vector = near_null[group * step + i, s, t, low:high, :].astype(F32)
                        for n in range(RHS):
                            term = vector[:8] * halves[n][0] + vector[8:] * halves[n][1]
                            key = (i, n, block)
                            totals[key] = term if key not in totals else totals[key] + term
        for (i, n, block), value in totals.items():
            place = 8 * (48 * n + 2 * (group * step + i) + block)
            sums[pl.ds(pl.multiple_of(place, 8), 8), :] = value
        return carry

    lax.fori_loop(0, NVEC // group, vectors, 0)
    count = 2 * NVEC * RHS
    fold = jnp.where(
        lax.broadcasted_iota(I32, (count, 8 * count), 1) >> 3 == lax.broadcasted_iota(I32, (count, 8 * count), 0), 1.0, 0.0
    ).astype(BF16)
    spread = jnp.where(
        lax.broadcasted_iota(I32, (LANES, LANES), 0) >> 2 == lax.broadcasted_iota(I32, (LANES, LANES), 1) & 31, 1.0, 0.0
    ).astype(BF16)
    rhs = exact_sum(spread, exact_sum(fold, sums[...], True), False)
    out_rhs[...] = rhs
    out_rounded[...] = rhs.astype(BF16)


def coarse_step(scal, operator, rhs, estimate, rounded, ta, tb, xa, xb, beside, out):
    row, lane = tile_iotas()
    t_odd, x_odd = scal[T_INDEX] & 1, scal[X_INDEX] & 1
    even_row = (row & 1) == 0
    for i in range(12):
        where = slice(8 * i, 8 * i + 8)
        own = rounded[where].astype(F32)
        t_first, t_second = ta[where].astype(F32), tb[where].astype(F32)
        x_first, x_second = xa[where].astype(F32), xb[where].astype(F32)
        beside[0, where] = own
        beside[1, where] = jnp.where(t_odd == 0, t_first, t_second)
        beside[2, where] = jnp.where(t_odd == 0, t_second, t_first)
        after = jnp.where(x_odd == 0, x_first, x_second)
        before = jnp.where(x_odd == 0, x_second, x_first)
        own_up, own_down = roll(own, 7, 0), roll(own, 1, 0)
        beside[3, where] = jnp.where(even_row, own_up, roll(after, 1, 0))
        beside[4, where] = jnp.where(even_row, roll(before, 7, 0), own_down)
        beside[5, where] = roll(own, LANES - 1, 1)
        beside[6, where] = roll(own, 1, 1)
    totals = [[None] * RHS for _ in range(6)]
    for b in range(7):
        near = [[beside[b, 48 * n + 8 * j : 48 * n + 8 * j + 8, :] for j in range(6)] for n in range(RHS)]
        for kk in range(6):
            for j in range(6):
                block = operator[b, kk, 8 * j : 8 * j + 8, :]
                for n in range(RHS):
                    term = block * near[n][j]
                    totals[kk][n] = term if totals[kk][n] is None else totals[kk][n] + term
    diagonal = (lane >> 5) == (row >> 1)
    for n in range(RHS):
        for kk in range(6):
            where = slice(48 * n + 8 * kk, 48 * n + 8 * kk + 8)
            value = totals[kk][n]
            value = value + roll(value, 4, 0)
            value = value + roll(value, 2, 0)
            value = jnp.where(diagonal, value, 0.0)
            value = value + roll(value, 64, 1)
            value = value + roll(value, 32, 1)
            out[where] = estimate[where] + (rhs[where] - value)


def coarse_kernel(scal, operator, rhs, estimate, rounded, ta, tb, xa, xb, out, out_rounded, beside):
    coarse_step(scal, operator, rhs, estimate, rounded, ta, tb, xa, xb, beside, out)
    out_rounded[...] = out[...].astype(BF16)


def prolong_kernel(
    scal, operator, rhs, estimate, rounded, ta, tb, xa, xb, near_null, solution,
    out, t_a, t_b, x_a, x_b,
    beside, final, spread_rows,
):
    coarse_step(scal, operator, rhs, estimate, rounded, ta, tb, xa, xb, beside, final)
    widen = jnp.where(
        lax.broadcasted_iota(I32, (LANES, LANES), 0) == lax.broadcasted_iota(I32, (LANES, LANES), 1) >> 2, 1.0, 0.0
    ).astype(BF16)
    wide = jnp.dot(final[...].astype(BF16), widen, preferred_element_type=F32)
    for i in range(2 * NVEC * RHS):
        spread_rows[i] = jnp.broadcast_to(wide[i : i + 1, :], (8, LANES))

    def body(step, carry):
        s, t = step // LT, step % LT
        for block in range(2):
            low, mid, high = 16 * block, 16 * block + 8, 16 * block + 16
            totals = [None] * RHS
            for k in range(NVEC):
                vector = near_null[k, s, t, low:high, :].astype(F32)
                for n in range(RHS):
                    weight = spread_rows[48 * n + 2 * k + block]
                    term = (vector[:8] * weight, vector[8:] * weight)
                    old = totals[n]
                    totals[n] = term if old is None else (old[0] + term[0], old[1] + term[1])
            for n in range(RHS):
                for part, span in enumerate((slice(low, mid), slice(mid, high))):
                    out[2 * s + n, t, span, :] = solution[2 * s + n, t, span, :] + totals[n][part]
        return carry

    lax.fori_loop(0, 4 * LT, body, 0)
    first = lax.broadcasted_iota(I32, (8, LANES), 0) < 4
    pack_shares(scal, 8, lambda c, t: out[c, t], t_a, t_b, x_a, x_b, first)


def post_kernel(
    scal, source, mass, links, ta, tb, xa, xb, ca, cb, solution, sta, stb, sxa, sxb, sca, scb,
    out, t_face_a, t_face_b, x_face_a, x_face_b,
    src, signs, inverse, field_a, field_b,
):
    row, lane = tile_iotas()
    fill_inputs(scal, source, mass, links, (ta, tb, xa, xb, ca, cb), src, signs, inverse)

    def put(c, t, rows, value):
        field_a[c, t, rows, :] = value

    def add_low(c, t, rows, value):
        field_a[c, t, rows, :] = field_a[c, t, rows, :] + value

    put_halos(scal, 8, sta, stb, sxa, sxb, sca, scb, put, add_low, row < 4)

    def own_slice(t, carry):
        for c in range(8):
            field_a[c, t + 4, PAD + 16 : PAD + 48, :] = solution[c, t]
        return carry

    lax.fori_loop(0, LT, own_slice, 0)
    three_sweeps(scal, 4, field_a, field_b, src, signs, inverse, row, lane)
    half_sweep(scal, 7, field_a, field_b, src, signs, inverse, (4, 8), (2, 6), row, lane)

    def finish(t, carry):
        for c in range(8):
            out[c, t] = field_a[c, t + 4, PAD + 16 : PAD + 48, :]
        return carry

    lax.fori_loop(0, LT, finish, 0)
    t_odd, x_odd = scal[T_INDEX] & 1, scal[X_INDEX] & 1
    for face, low_side in ((t_face_a, t_odd), (t_face_b, 1 - t_odd)):
        t = 3 * (1 - low_side)
        factor = (1 - 2 * low_side).astype(F32)
        for s in range(2):
            for n in range(RHS):
                face[2 * s + n] = out[2 * s + n, t] + factor * out[2 * (s + 2) + n, t]
    for face, low_side in ((x_face_a, x_odd), (x_face_b, 1 - x_odd)):
        where = pl.ds(pl.multiple_of(24 * (1 - low_side), 8), 8)
        factor = (1 - 2 * low_side).astype(F32)
        for n in range(RHS):
            for t in range(LT):
                face[n, t] = out[n, t, where, :] + factor * out[2 + n, t, where, :]
                face[2 + n, t] = out[4 + n, t, where, :] - factor * out[6 + n, t, where, :]


def residual_kernel(scal, source, mass, links, solution, ta, tb, xa, xb, out, signs, field):
    row, lane = tile_iotas()
    t_odd, x_odd = scal[T_INDEX] & 1, scal[X_INDEX] & 1
    own = slice(PAD, PAD + ROWS)
    zero = jnp.zeros((ROWS, LANES), F32)

    def own_slice(t, carry):
        for c in range(8):
            field[c, t + 1, own, :] = solution[c, t]
        for m in range(4):
            scale = 2.0 if m == 2 else 1.0
            signs[m, t + 1, own, :] = scale * (0.5 - links[m, t].astype(F32))
        return carry

    lax.fori_loop(0, LT, own_slice, 0)
    for face, low_side in ((ta, t_odd), (tb, 1 - t_odd)):
        t = 5 * (1 - low_side)
        for c in range(4):
            field[c, t, own, :] = face[c]
            field[c + 4, t, own, :] = zero
    for face, low_side in ((xa, x_odd), (xb, 1 - x_odd)):
        where = pl.ds(pl.multiple_of((PAD + ROWS) * (1 - low_side), 8), 8)
        for t in range(LT):
            for n in range(RHS):
                field[n, t + 1, where, :] = face[n, t]
                field[2 + n, t + 1, where, :] = zero[:8]
                field[4 + n, t + 1, where, :] = face[2 + n, t]
                field[6 + n, t + 1, where, :] = zero[:8]

    def put(t, tile, side, centre, hop):
        where = slice(8 * tile, 8 * tile + 8)
        diag = 4.0 + mass[t - 1, where, :]
        for s in range(4):
            c = 2 * s + side
            out[c, t - 1, where, :] = (source[c, t - 1, where, :] - diag * centre[s]) + hop[s]

    visit(field, signs, (1, 5), (0, 4), put, row)


def call(kernel, mebibytes, outs, scratch, *args):
    return pl.pallas_call(
        kernel,
        out_shape=outs,
        in_specs=[SM] + [VM] * (len(args) - 1),
        out_specs=[VM] * len(outs),
        scratch_shapes=[pltpu.VMEM(dims, F32) for dims in scratch],
        compiler_params=params(mebibytes),
    )(*args)


def swap(values, axis, odd_pairs):
    devices = lax.axis_size(axis)
    if odd_pairs:
        pairs = [(i, (i + 1) % devices if i % 2 else (i - 1) % devices) for i in range(devices)]
    else:
        pairs = [(i, i ^ 1) for i in range(devices)]
    return lax.ppermute(values, axis, pairs)


def swap_four(t_first, t_second, x_first, x_second):
    return (
        swap(t_first, "ta", False),
        swap(t_second, "ta", True),
        swap(x_first, "xyz", False),
        swap(x_second, "xyz", True),
    )


def share_shapes(fields):
    slabs = fields * LT + 8
    return [shape((slabs, rows, LANES), BF16) for rows in (ROWS, ROWS, 16, 16)]


def exchange(scal, fields, shares):
    ta, tb, xa, xb = swap_four(*shares)
    corners = call(corner_kernel, 4, [shape((2 * fields, ROWS, LANES), BF16)] * 2, [], scal, xa, xb)
    return ta, tb, xa, xb, swap(corners[0], "ta", False), swap(corners[1], "ta", True)


def per_device(source, mass, links, near_null, coarse_op, plan):
    out_shape = source.shape
    source = source.reshape(8, LT, ROWS, LANES)
    mass = mass.reshape(LT, ROWS, LANES)
    links = links.reshape(4, LT, ROWS, LANES)
    near_null = near_null.reshape(NVEC, 4, LT, ROWS, LANES)
    coarse_op = coarse_op.reshape(9, NVEC, 2 * NVEC, 32)
    scal = jnp.concatenate([plan, jnp.stack([lax.axis_index("ta"), lax.axis_index("xyz")]).astype(I32)])
    count = 2 * NVEC * RHS
    ext = [(8, ET, EROWS, LANES), (4, ET, EROWS, LANES), (ET, EROWS, LANES)] + [(8, ET, EROWS, LANES)] * 2

    shares = call(pack_kernel, 6, share_shapes(FIELDS), [], scal, source, mass, links)
    halos = exchange(scal, FIELDS, shares)
    operator = pl.pallas_call(
        relayout_kernel,
        out_shape=shape((7, 6, 2 * NVEC, LANES), F32),
        in_specs=[VM],
        out_specs=VM,
        compiler_params=params(12),
        cost_estimate=pl.CostEstimate(flops=1 << 20, bytes_accessed=1 << 22, transcendentals=0),
    )(coarse_op)
    field = (8, LT, ROWS, LANES)
    solution, rhs, rounded = call(
        pre_kernel,
        28,
        [shape(field, F32), shape((count, LANES), F32), shape((count, LANES), BF16)],
        ext + [field, (8 * count, LANES)],
        scal, source, mass, links, *halos, near_null,
    )
    estimate = rhs
    beside = (7, count, LANES)
    for turn in range(1, KC):
        near = swap_four(rounded, rounded, rounded, rounded)
        given = (scal, operator, rhs, estimate, rounded, *near)
        if turn < KC - 1:
            outs = [shape((count, LANES), F32), shape((count, LANES), BF16)]
            estimate, rounded = call(coarse_kernel, 6, outs, [beside], *given)
    outs = [shape(field, F32)] + share_shapes(8)
    solution, *shares = call(
        prolong_kernel, 12, outs, [beside, (count, LANES), (count, 8, LANES)], *given, near_null, solution
    )
    fine = exchange(scal, 8, shares)
    t_face, x_face = shape((4, ROWS, LANES), F32), shape((4, LT, 8, LANES), F32)
    solution, *faces = call(
        post_kernel,
        28,
        [shape(field, F32), t_face, t_face, x_face, x_face],
        ext,
        scal, source, mass, links, *halos, solution, *fine,
    )
    near = swap_four(*faces)
    (residual,) = call(
        residual_kernel, 8, [shape(field, F32)], [(4, 6, 48, LANES), (8, 6, 48, LANES)],
        scal, source, mass, links, solution, *near,
    )
    return solution.reshape(out_shape), residual.reshape(out_shape)


def solution(mesh):
    return jax.shard_map(
        per_device,
        mesh=mesh,
        in_specs=(
            P(None, None, "ta", "xyz", None, None),
            P("ta", "xyz", None, None),
            P(None, "ta", "xyz", None, None),
            P(None, None, "ta", "xyz", None, None),
            P(None, None, None, "ta", "xyz", None, None),
            P(),
        ),
        out_specs=(P(None, None, "ta", "xyz", None, None), P(None, None, "ta", "xyz", None, None)),
        check_vma=False,
    )
```

```python
import functools

import jax
import jax.numpy as jnp
from jax import lax
from jax.experimental import pallas as pl
from jax.experimental.pallas import tpu as pltpu
from jax.sharding import PartitionSpec as P

LT, ROWS, LANES = 4, 32, 128
NVEC, RHS, KC, SWEEPS = 24, 2, 6, 8
ET, EROWS, PAD = 14, 80, 8
T0, OWN = 5, slice(24, 56)
FIELDS = 13
F32, BF16, I32 = jnp.float32, jnp.bfloat16, jnp.int32


def params(mebibytes):
    return pltpu.CompilerParams(vmem_limit_bytes=int(mebibytes * 1024 * 1024))


def shape(dims, dtype):
    return jax.ShapeDtypeStruct(dims, dtype)


VM = pl.BlockSpec(memory_space=pltpu.VMEM)
HB = pl.BlockSpec(memory_space=pltpu.HBM)


def roll(values, shift, axis):
    return pltpu.roll(values, shift, axis)


def tile_iotas():
    row = lax.broadcasted_iota(I32, (8, LANES), 0)
    lane = lax.broadcasted_iota(I32, (8, LANES), 1)
    return row, lane


def x_pair(spins):
    ahead = (spins[0] - spins[1], spins[2] + spins[3])
    behind = (spins[0] + spins[1], spins[2] - spins[3])
    return [roll(value, 4, 0) for value in ahead + behind]


def hops(centre, before, after, ahead_t, behind_t, coefs, row):
    first = row < 4
    top = (row & 3) == 0
    bottom = (row & 3) == 3
    sign_t, sign_x, sign_y, sign_z = coefs
    p0, p1 = ahead_t[0] - ahead_t[2], ahead_t[1] - ahead_t[3]
    q0, q1 = behind_t[0] + behind_t[2], behind_t[1] + behind_t[3]
    along_t = (q0 + p0, q1 + p1, q0 - p0, q1 - p1)
    here = centre[1]
    u0, u2 = (jnp.where(first, here[i], after[i]) for i in (0, 1))
    w0, w2 = (jnp.where(first, before[i], here[i]) for i in (2, 3))
    along_x = (w0 + u0, w0 - u0, u2 + w2, u2 - w2)
    v = centre[0]

    def back(value):
        return jnp.where(top, roll(value, 5, 0), roll(value, 1, 0))

    def forth(value):
        return jnp.where(bottom, roll(value, 3, 0), roll(value, 7, 0))

    along_y = (back(v[0]), forth(v[1]), forth(v[2]), back(v[3]))
    f, g = roll(v[0] + v[3], LANES - 1, 1), roll(v[1] - v[2], LANES - 1, 1)
    h, k = roll(v[0] - v[3], 1, 1), roll(v[1] + v[2], 1, 1)
    along_z = (f + h, k + g, k - g, f - h)
    return [
        (sign_t * along_t[s] + sign_x * along_x[s]) + (sign_y * along_y[s] + sign_z * along_z[s])
        for s in range(4)
    ]


def visit(field, signs, slices, tiles, put, row):
    lows = slices[0::2]
    length = slices[1] - slices[0]

    def body(step, carry):
        t = step + lows[0] if len(lows) == 1 else jnp.where(step < length, step + lows[0], step - length + lows[1])

        def spins_at(time, tile, side):
            start = PAD + 8 * tile
            return [field[2 * s + side, time, start : start + 8, :] for s in range(4)]

        for side in range(RHS):
            spins = {}
            pairs = {}
            for tile in range(tiles[0] - 1, tiles[1] + 1):
                spins[tile] = spins_at(t, tile, side)
                pairs[tile] = x_pair(spins[tile])
            for tile in range(*tiles):
                start = PAD + 8 * tile
                coefs = [signs[m, t, start : start + 8, :] for m in range(4)]
                sums = hops(
                    (spins[tile], pairs[tile]),
                    pairs[tile - 1],
                    pairs[tile + 1],
                    spins_at(t + 1, tile, side),
                    spins_at(t - 1, tile, side),
                    coefs,
                    row,
                )
                put(t, tile, side, spins[tile], sums)
        return carry

    lax.fori_loop(0, length * len(lows), body, 0)


def chosen(plan, colour, t, tile, lane):
    block = lax.axis_index("ta") + (t + 3) // 4 + tile // 2 + 1
    return ((lane >> 2) & 1) == ((plan[colour] + block) & 1)


def half_sweep(plan, colour, target, field, source, signs, inverse, slices, tiles, row, lane):
    def put(t, tile, side, centre, sums):
        start = PAD + 8 * tile
        mask = chosen(plan, colour, t, tile, lane)
        scale = inverse[t, start : start + 8, :]
        for s in range(4):
            value = (source[2 * s + side, t, start : start + 8, :] + sums[s]) * scale
            target[2 * s + side, t, start : start + 8, :] = jnp.where(mask, value, centre[s])

    visit(field, signs, slices, tiles, put, row)


def wide_sweep(plan, colour, depth, target, field, src, signs, inverse, row, lane):
    done = 0
    while done <= depth:
        tiles = (2, 6) if depth == done else (1, 7) if depth - done <= 2 else (0, 8)
        last = depth if depth == done else depth - 1 if depth - done <= 2 else depth - 3
        if done == 0:
            slices = (T0 - last, T0 + LT + last)
        else:
            slices = (T0 - last, T0 - done + 1, T0 + LT + done - 1, T0 + LT + last)
        half_sweep(plan, colour, target, field, src, signs, inverse, slices, tiles, row, lane)
        done = last + 1


def places():
    t_odd, x_odd = lax.axis_index("ta") & 1, lax.axis_index("xyz") & 1
    return (t_odd, 1 - t_odd), (x_odd, 1 - x_odd)


def x_start(before):
    return pl.multiple_of(PAD + 48 * (1 - before), 8)


def column_of(data, t, before, first):
    pair = data[8 * (t // 2) : 8 * (t // 2) + 8]
    turned = roll(pair, 4, 0)
    top, bottom = (pair, turned) if t % 2 == 0 else (turned, pair)
    return jnp.where(before == 0, jnp.where(first, top, 0.0), jnp.where(first, 0.0, bottom))


def put_cross(fields, ta, tb, xa, xb, put, add_low, first):
    t_before, x_before = places()
    for data, before in ((ta, t_before[0]), (tb, t_before[1])):
        for part in range(2):
            base = T0 + LT - 8 * before + 2 * part

            def t_slice(t, carry, data=data[part], base=base):
                for c in range(fields):
                    put(c, base + t, OWN, data[fields * t + c].astype(F32))
                return carry

            lax.fori_loop(0, 2, t_slice, 0)
        near = T0 + LT - 5 * before
        for c in range(8):
            add_low(c, near, OWN, data[c // 4][2 * fields + c % 4].astype(F32))
    for data, before in ((xa, x_before[0]), (xb, x_before[1])):
        start = x_start(before)

        def x_slice(t, carry, data=data, start=start):
            for c in range(fields):
                put(c, T0 + t, pl.ds(start, 16), data[fields * t + c].astype(F32))
            return carry

        lax.fori_loop(0, LT, x_slice, 0)
        where = pl.ds(pl.multiple_of(start + 8 * before, 8), 8)
        for c in range(8):
            low = data[4 * fields + c].astype(F32)
            for t in range(LT):
                add_low(c, T0 + t, where, column_of(low, t, before, first))


def put_corners(fields, ca, cb, put, deep):
    t_before, x_before = places()
    for data, before in ((ca, t_before[0]), (cb, t_before[1])):
        near, step = T0 + LT - 5 * before, 1 - 2 * before
        for half in range(2):
            start = x_start(x_before[half])
            facing = pl.ds(pl.multiple_of(start + 8 * x_before[half], 8), 8)
            part = slice(16 * half, 16 * half + 16)
            for c in range(fields):
                put(c, near, pl.ds(start, 16), data[c, part, :].astype(F32))
                if deep:
                    put(c, near + step, pl.ds(start, 16), data[fields + c, part, :].astype(F32))
                value = data[(1 + deep) * fields + c, part, :].astype(F32)
                put(c, near + (1 + deep) * step, facing, value[:8])
                put(c, near + (2 + deep) * step, facing, value[8:])
        if deep:
            for c in range(fields):
                put(c, (ET - 1) * (1 - before), OWN, data[3 * fields + c].astype(F32))


def low_part(value):
    return value - value.astype(BF16).astype(F32)


def pack_t(fields, read, t_a, t_b):
    t_before, _ = places()
    for part in range(2):

        def one_slice(t, carry, part=part):
            for c in range(fields):
                value = read(c, 2 * part + t).astype(BF16)
                t_a[part][fields * t + c] = value
                t_b[part][fields * t + c] = value
            return carry

        lax.fori_loop(0, 2, one_slice, 0)
    for c in range(8):
        for out, before in ((t_a, t_before[0]), (t_b, t_before[1])):
            out[c // 4][2 * fields + c % 4] = low_part(read(c, 3 * (1 - before))).astype(BF16)


def pack_x(fields, read, x_a, x_b, first):
    _, x_before = places()

    def one_slice(t, carry):
        for c in range(fields):
            value = read(c, t).astype(BF16)
            x_a[fields * t + c] = jnp.where(x_before[0] == 0, value[16:], value[:16])
            x_b[fields * t + c] = jnp.where(x_before[1] == 0, value[16:], value[:16])
        return carry

    lax.fori_loop(0, LT, one_slice, 0)

    def join(tops, bottoms):
        return jnp.concatenate([jnp.where(first, tops[t], bottoms[t + 1]) for t in (0, 2)], 0)

    def turn(values):
        return [roll(value, 4, 0) for value in values]

    for c in range(8):
        values = [read(c, t) for t in range(LT)]
        lows = [low_part(value[:8]) for value in values]
        highs = [low_part(value[24:]) for value in values]
        low, high = join(lows, turn(lows)), join(turn(highs), highs)
        for out, before in ((x_a, x_before[0]), (x_b, x_before[1])):
            out[4 * fields + c] = jnp.where(before == 0, high, low).astype(BF16)
        if x_a.shape[0] > 4 * fields + 8:
            lows = [value[16:24] for value in values]
            highs = [value[8:16] for value in values]
            low, high = join(lows, turn(lows)), join(turn(highs), highs)
            for out, before in ((x_a, x_before[0]), (x_b, x_before[1])):
                out[4 * fields + 8 + c] = jnp.where(before == 0, high, low).astype(BF16)


def corner_kernel(fields, deep, *refs):
    xa, xb, *beyond, ca, cb = refs
    t_before, x_before = places()
    for out, before, behind in ((ca, t_before[0], beyond[2:]), (cb, t_before[1], beyond[:2])):
        if deep:
            for c in range(fields):
                out[3 * fields + c] = jnp.where(before == 1, behind[0][c], behind[1][fields + c])
        near, step = 3 * (1 - before), 2 * before - 1

        def one_field(c, carry, out=out, near=near, step=step):
            for half, data in enumerate((xa, xb)):
                where = slice(16 * half, 16 * half + 16)
                for depth in range(1 + deep):
                    out[depth * fields + c, where, :] = data[fields * (near + depth * step) + c]
                pieces = []
                for depth in (1 + deep, 2 + deep):
                    value = data[fields * (near + depth * step) + c].astype(F32)
                    pieces.append(jnp.where(x_before[half] == 0, value[:8], value[8:]))
                out[(1 + deep) * fields + c, where, :] = jnp.concatenate(pieces, 0).astype(BF16)
            return carry

        lax.fori_loop(0, fields, one_field, 0)


def input_reader(source, mass, links):
    def read(c, t):
        if c < 8:
            return source[c, t]
        if c == 8:
            return mass[t]
        return (1.0 if c == 11 else 0.5) * (1 - 2 * links[c - 9, t]).astype(F32)

    return read


def input_writer(src, signs, inverse):
    def put(c, t, rows, value):
        if c < 8:
            src[c, t, rows, :] = value
        elif c == 8:
            inverse[t, rows, :] = 1.0 / (4.0 + value)
        else:
            signs[c - 9, t, rows, :] = value

    return put


def adder(field):
    def add_low(c, t, rows, value):
        field[c, t, rows, :] = field[c, t, rows, :] + value

    return add_low


def load_kernel(source, mass, links, source_out, mass_out, links_out, x_a, x_b, sems):
    pairs = ((source, source_out), (mass, mass_out), (links, links_out))
    copies = [pltpu.make_async_copy(a, b, sems.at[i]) for i, (a, b) in enumerate(pairs)]
    for copy in copies:
        copy.start()
    for copy in copies:
        copy.wait()
    first = lax.broadcasted_iota(I32, (8, LANES), 0) < 4
    pack_x(FIELDS, input_reader(source_out, mass_out, links_out), x_a, x_b, first)


def share_kernel(source, mass, links, *shares):
    pack_t(FIELDS, input_reader(source, mass, links), shares[:2], shares[2:])


def cross_kernel(source, mass, links, ta1, ta2, tb1, tb2, xa, xb, src, signs, inverse):
    read, put = input_reader(source, mass, links), input_writer(src, signs, inverse)

    def own_slice(t, carry):
        for c in range(FIELDS):
            put(c, t + T0, OWN, read(c, t))
        return carry

    lax.fori_loop(0, LT, own_slice, 0)
    first = lax.broadcasted_iota(I32, (8, LANES), 0) < 4
    put_cross(FIELDS, (ta1, ta2), (tb1, tb2), xa, xb, put, adder(src), first)


def relayout_kernel(operator, result):
    def group(kk, carry):
        def block(b, q):
            return operator[b, 4 * kk + q].astype(F32)

        for place, kinds in enumerate(((0, 5, 6), (1,), (2,), (3,), (4,), (7,), (8,))):
            pieces = []
            for q in range(4):
                piece = block(kinds[0], q)
                for b in kinds[1:]:
                    piece = piece + block(b, q)
                pieces.append(piece)
            result[place, kk] = jnp.concatenate(pieces, axis=-1)
        return carry

    lax.fori_loop(0, 6, group, 0)


def exact_sum(matrix, values, left):
    high = values.astype(BF16)
    low = (values - high.astype(F32)).astype(BF16)

    def one(part):
        pair = (matrix, part) if left else (part, matrix)
        return jnp.dot(*pair, preferred_element_type=F32)

    return one(high) + one(low)


def pre_kernel(
    plan_far, mass, ca, cb, src_in, signs_in, inverse_in, near_null,
    out_solution, out_rhs, out_rounded, src, signs, inverse,
    field_a, field_b, resid, sums, plan, sem,
):
    del src_in, signs_in, inverse_in
    plan_copy = pltpu.make_async_copy(plan_far, plan, sem)
    plan_copy.start()
    row, lane = tile_iotas()
    put_corners(FIELDS, ca, cb, input_writer(src, signs, inverse), 0)
    plan_copy.wait()

    def first_sweep(t, carry):
        for tile in range(8):
            start = PAD + 8 * tile
            mask = chosen(plan, 0, t, tile, lane)
            scale = jnp.where(mask, inverse[t, start : start + 8, :], 0.0)
            for c in range(8):
                field_a[c, t, start : start + 8, :] = src[c, t, start : start + 8, :] * scale
        return carry

    lax.fori_loop(1, ET - 1, first_sweep, 0)
    common = (src, signs, inverse, row, lane)
    wide_sweep(plan, 1, 3, field_b, field_a, *common)
    wide_sweep(plan, 2, 2, field_a, field_b, *common)
    wide_sweep(plan, 3, 1, field_b, field_a, *common)

    def put(t, tile, side, centre, hop):
        start = PAD + 8 * tile
        inner = 8 * (tile - 2)
        diag = 4.0 + mass[t - T0, inner : inner + 8, :]
        for s in range(4):
            c = 2 * s + side
            value = (src[c, t, start : start + 8, :] - diag * centre[s]) + hop[s]
            resid[c, t - T0, inner : inner + 8, :] = value.astype(BF16).astype(F32)
            out_solution[c, t - T0, inner : inner + 8, :] = centre[s]

    visit(field_b, signs, (T0, T0 + LT), (2, 6), put, row)
    group = 4

    def vectors(step, carry):
        totals = {}
        for s in range(4):
            for t in range(LT):
                for block in range(2):
                    low, mid, high = 16 * block, 16 * block + 8, 16 * block + 16
                    halves = [
                        (resid[2 * s + n, t, low:mid, :], resid[2 * s + n, t, mid:high, :]) for n in range(RHS)
                    ]
                    for i in range(group):
                        vector = near_null[group * step + i, s, t, low:high, :].astype(F32)
                        for n in range(RHS):
                            term = vector[:8] * halves[n][0] + vector[8:] * halves[n][1]
                            key = (i, n, block)
                            totals[key] = term if key not in totals else totals[key] + term
        for (i, n, block), value in totals.items():
            place = 8 * (48 * n + 2 * (group * step + i) + block)
            sums[pl.ds(pl.multiple_of(place, 8), 8), :] = value
        return carry

    lax.fori_loop(0, NVEC // group, vectors, 0)
    count = 2 * NVEC * RHS
    fold = jnp.where(
        lax.broadcasted_iota(I32, (count, 8 * count), 1) >> 3 == lax.broadcasted_iota(I32, (count, 8 * count), 0), 1.0, 0.0
    ).astype(BF16)
    spread = jnp.where(
        lax.broadcasted_iota(I32, (LANES, LANES), 0) >> 2 == lax.broadcasted_iota(I32, (LANES, LANES), 1) & 31, 1.0, 0.0
    ).astype(BF16)
    rhs = exact_sum(spread, exact_sum(fold, sums[...], True), False)
    out_rhs[...] = rhs
    out_rounded[...] = rhs.astype(BF16)


def coarse_step(operator, rhs, estimate, rounded, ta, tb, xa, xb, beside, out):
    row, lane = tile_iotas()
    t_odd, x_odd = lax.axis_index("ta") & 1, lax.axis_index("xyz") & 1
    even_row = (row & 1) == 0
    for i in range(12):
        where = slice(8 * i, 8 * i + 8)
        own = rounded[where].astype(F32)
        t_first, t_second = ta[where].astype(F32), tb[where].astype(F32)
        x_first, x_second = xa[where].astype(F32), xb[where].astype(F32)
        beside[0, where] = own
        beside[1, where] = jnp.where(t_odd == 0, t_first, t_second)
        beside[2, where] = jnp.where(t_odd == 0, t_second, t_first)
        after = jnp.where(x_odd == 0, x_first, x_second)
        before = jnp.where(x_odd == 0, x_second, x_first)
        own_up, own_down = roll(own, 7, 0), roll(own, 1, 0)
        beside[3, where] = jnp.where(even_row, own_up, roll(after, 1, 0))
        beside[4, where] = jnp.where(even_row, roll(before, 7, 0), own_down)
        beside[5, where] = roll(own, LANES - 1, 1)
        beside[6, where] = roll(own, 1, 1)
    totals = [[None] * RHS for _ in range(6)]
    for b in range(7):
        near = [[beside[b, 48 * n + 8 * j : 48 * n + 8 * j + 8, :] for j in range(6)] for n in range(RHS)]
        for kk in range(6):
            for j in range(6):
                block = operator[b, kk, 8 * j : 8 * j + 8, :]
                for n in range(RHS):
                    term = block * near[n][j]
                    totals[kk][n] = term if totals[kk][n] is None else totals[kk][n] + term
    diagonal = (lane >> 5) == (row >> 1)
    for n in range(RHS):
        for kk in range(6):
            where = slice(48 * n + 8 * kk, 48 * n + 8 * kk + 8)
            value = totals[kk][n]
            value = value + roll(value, 4, 0)
            value = value + roll(value, 2, 0)
            value = jnp.where(diagonal, value, 0.0)
            value = value + roll(value, 64, 1)
            value = value + roll(value, 32, 1)
            out[where] = estimate[where] + (rhs[where] - value)


def coarse_kernel(operator, rhs, estimate, rounded, ta, tb, xa, xb, out, out_rounded, beside):
    coarse_step(operator, rhs, estimate, rounded, ta, tb, xa, xb, beside, out)
    out_rounded[...] = out[...].astype(BF16)


def prolong_kernel(
    operator, rhs, estimate, rounded, ta, tb, xa, xb, near_null, solution,
    out, x_a, x_b,
    beside, final, spread_rows,
):
    coarse_step(operator, rhs, estimate, rounded, ta, tb, xa, xb, beside, final)
    widen = jnp.where(
        lax.broadcasted_iota(I32, (LANES, LANES), 0) == lax.broadcasted_iota(I32, (LANES, LANES), 1) >> 2, 1.0, 0.0
    ).astype(BF16)
    wide = jnp.dot(final[...].astype(BF16), widen, preferred_element_type=F32)
    for i in range(2 * NVEC * RHS):
        spread_rows[i] = jnp.broadcast_to(wide[i : i + 1, :], (8, LANES))

    def body(step, carry):
        s, t = step // LT, step % LT
        for block in range(2):
            low, mid, high = 16 * block, 16 * block + 8, 16 * block + 16
            totals = [None] * RHS
            for k in range(NVEC):
                vector = near_null[k, s, t, low:high, :].astype(F32)
                for n in range(RHS):
                    weight = spread_rows[48 * n + 2 * k + block]
                    term = (vector[:8] * weight, vector[8:] * weight)
                    old = totals[n]
                    totals[n] = term if old is None else (old[0] + term[0], old[1] + term[1])
            for n in range(RHS):
                for part, span in enumerate((slice(low, mid), slice(mid, high))):
                    out[2 * s + n, t, span, :] = solution[2 * s + n, t, span, :] + totals[n][part]
        return carry

    lax.fori_loop(0, 4 * LT, body, 0)
    first = lax.broadcasted_iota(I32, (8, LANES), 0) < 4
    pack_x(8, lambda c, t: out[c, t], x_a, x_b, first)


def share_field_kernel(solution, *shares):
    pack_t(8, lambda c, t: solution[c, t], shares[:2], shares[2:])


def field_kernel(solution, ta1, ta2, tb1, tb2, xa, xb, field):
    def put(c, t, rows, value):
        field[c, t, rows, :] = value

    def own_slice(t, carry):
        for c in range(8):
            field[c, t + T0, OWN, :] = solution[c, t]
        return carry

    lax.fori_loop(0, LT, own_slice, 0)
    first = lax.broadcasted_iota(I32, (8, LANES), 0) < 4
    put_cross(8, (ta1, ta2), (tb1, tb2), xa, xb, put, adder(field), first)
    _, x_before = places()
    for data, before in ((xa, x_before[0]), (xb, x_before[1])):
        where = pl.ds(pl.multiple_of((EROWS - 8) * (1 - before), 8), 8)
        for c in range(8):
            layer = data[40 + c].astype(F32)
            for t in range(LT):
                put(c, T0 + t, where, column_of(layer, t, before, first))


def post_kernel(
    plan_far, mass, src, signs, inverse, field_in, ca, cb, out, residual, field_a, field_b, plan, sem
):
    del field_in
    plan_copy = pltpu.make_async_copy(plan_far, plan, sem)
    plan_copy.start()
    row, lane = tile_iotas()

    def put_field(c, t, rows, value):
        field_a[c, t, rows, :] = value

    put_corners(8, ca, cb, put_field, 1)
    plan_copy.wait()
    common = (src, signs, inverse, row, lane)
    wide_sweep(plan, 4, 4, field_b, field_a, *common)
    wide_sweep(plan, 5, 3, field_a, field_b, *common)
    wide_sweep(plan, 6, 2, field_b, field_a, *common)
    wide_sweep(plan, 7, 1, field_a, field_b, *common)

    def put(t, tile, side, centre, hop):
        start, inner = PAD + 8 * tile, 8 * (tile - 2)
        where = slice(inner, inner + 8)
        diag = 4.0 + mass[t - T0, where, :]
        for s in range(4):
            c = 2 * s + side
            out[c, t - T0, where, :] = centre[s]
            residual[c, t - T0, where, :] = (src[c, t, start : start + 8, :] - diag * centre[s]) + hop[s]

    visit(field_a, signs, (T0, T0 + LT), (2, 6), put, row)


def call(kernel, mebibytes, outs, scratch, *args, aliases=(), far=(), cost=None):
    scratch = [item if not isinstance(item, tuple) else pltpu.VMEM(item, F32) for item in scratch]
    specs = [HB if i in far else VM for i in range(len(args))]
    return pl.pallas_call(
        kernel,
        out_shape=outs,
        in_specs=specs,
        out_specs=[VM] * len(outs),
        scratch_shapes=scratch,
        input_output_aliases=dict(aliases),
        compiler_params=params(mebibytes),
        cost_estimate=cost and pl.CostEstimate(flops=cost, bytes_accessed=cost, transcendentals=0),
    )(*args)


def swap(values, axis, odd_pairs):
    devices = lax.axis_size(axis)
    if odd_pairs:
        pairs = [(i, (i + 1) % devices if i % 2 else (i - 1) % devices) for i in range(devices)]
    else:
        pairs = [(i, i ^ 1) for i in range(devices)]
    return lax.ppermute(values, axis, pairs)


def swap_four(t_first, t_second, x_first, x_second):
    xb = swap(x_second, "xyz", True)
    xa = swap(x_first, "xyz", False)
    tb = swap(t_second, "ta", True)
    ta = swap(t_first, "ta", False)
    return ta, tb, xa, xb


def slabs(count, rows):
    return shape((count, rows, LANES), BF16)


def swap_six(ta1, ta2, tb1, tb2, x_first, x_second):
    xb = swap(x_second, "xyz", True)
    xa = swap(x_first, "xyz", False)
    second = [swap(part, "ta", True) for part in (tb1, tb2)]
    return *(swap(part, "ta", False) for part in (ta1, ta2)), *second, xa, xb


def corners_of(fields, deep, *near):
    kernel = functools.partial(corner_kernel, fields, deep)
    *t_parts, xa, xb = near
    beyond = t_parts if deep else ()
    ca, cb = call(kernel, 4, [slabs((2 + 2 * deep) * fields, ROWS)] * 2, [], xa, xb, *beyond)
    cb = swap(cb, "ta", True)
    return swap(ca, "ta", False), cb


def per_device(source, mass, links, near_null, coarse_op, plan):
    out_shape = source.shape
    source = source.reshape(8, LT, ROWS, LANES)
    mass = mass.reshape(LT, ROWS, LANES)
    links = links.reshape(4, LT, ROWS, LANES)
    near_null = near_null.reshape(NVEC, 4, LT, ROWS, LANES)
    coarse_op = coarse_op.reshape(9, NVEC, 2 * NVEC, 32)
    count = 2 * NVEC * RHS
    field, ext = (8, LT, ROWS, LANES), (8, ET, EROWS, LANES)
    inputs = [shape(ext, F32), shape((4, ET, EROWS, LANES), F32), shape((ET, EROWS, LANES), F32)]

    plan = pltpu.with_memory_space_constraint(plan, pltpu.HBM)
    source, mass, links, x_a, x_b = call(
        load_kernel,
        8,
        [shape(field, F32), shape(field[1:], F32), shape((4, *field[1:]), I32)] + [slabs(4 * FIELDS + 8, 16)] * 2,
        [pltpu.SemaphoreType.DMA((3,))],
        *(pltpu.with_memory_space_constraint(value, pltpu.HBM) for value in (source, mass, links)),
        far=(0, 1, 2),
    )
    shares = call(share_kernel, 6, [slabs(2 * FIELDS + 4, ROWS)] * 4, [], source, mass, links, cost=1 << 22)
    near = swap_six(*shares, x_a, x_b)
    corners = corners_of(FIELDS, 0, *near)
    src, signs, inverse = call(cross_kernel, 16, inputs, [], source, mass, links, *near, cost=1 << 22)
    operator = pl.pallas_call(
        relayout_kernel,
        out_shape=shape((7, 6, 2 * NVEC, LANES), F32),
        in_specs=[VM],
        out_specs=VM,
        compiler_params=params(12),
        cost_estimate=pl.CostEstimate(flops=1 << 20, bytes_accessed=1 << 22, transcendentals=0),
    )(coarse_op)
    solution, rhs, rounded, src, signs, inverse = call(
        pre_kernel,
        32,
        [shape(field, F32), shape((count, LANES), F32), shape((count, LANES), BF16)] + inputs,
        [ext, ext, field, (8 * count, LANES), pltpu.SMEM((SWEEPS,), I32), pltpu.SemaphoreType.DMA],
        plan, mass, *corners, src, signs, inverse, near_null,
        aliases=((4, 3), (5, 4), (6, 5)),
        far=(0,),
    )
    estimate = rhs
    beside = (7, count, LANES)
    for turn in range(1, KC):
        near = swap_four(rounded, rounded, rounded, rounded)
        given = (operator, rhs, estimate, rounded, *near)
        if turn < KC - 1:
            outs = [shape((count, LANES), F32), shape((count, LANES), BF16)]
            estimate, rounded = call(coarse_kernel, 6, outs, [beside], *given)
    solution, x_a, x_b = call(
        prolong_kernel,
        12,
        [shape(field, F32)] + [slabs(48, 16)] * 2,
        [beside, (count, LANES), (count, 8, LANES)],
        *given, near_null, solution,
    )
    shares = call(share_field_kernel, 4, [slabs(20, ROWS)] * 4, [], solution, cost=1 << 22)
    near = swap_six(*shares, x_a, x_b)
    corners = corners_of(8, 1, *near)
    (grown,) = call(field_kernel, 10, [shape(ext, F32)], [], solution, *near, cost=1 << 22)
    solution, residual, _ = call(
        post_kernel,
        28,
        [shape(field, F32)] * 2 + [shape(ext, F32)],
        [ext, pltpu.SMEM((SWEEPS,), I32), pltpu.SemaphoreType.DMA],
        plan, mass, src, signs, inverse, grown, *corners,
        aliases=((5, 2),),
        far=(0,),
    )
    return solution.reshape(out_shape), residual.reshape(out_shape)


def solution(mesh):
    return jax.shard_map(
        per_device,
        mesh=mesh,
        in_specs=(
            P(None, None, "ta", "xyz", None, None),
            P("ta", "xyz", None, None),
            P(None, "ta", "xyz", None, None),
            P(None, None, "ta", "xyz", None, None),
            P(None, None, None, "ta", "xyz", None, None),
            P(),
        ),
        out_specs=(P(None, None, "ta", "xyz", None, None), P(None, None, "ta", "xyz", None, None)),
        check_vma=False,
    )
```

```python
import functools

import jax
import jax.numpy as jnp
from jax import lax
from jax.experimental import pallas as pl
from jax.experimental.pallas import tpu as pltpu
from jax.sharding import PartitionSpec as P

LT, ROWS, LANES = 4, 32, 128
NVEC, RHS, KC, SWEEPS = 24, 2, 6, 8
ET, EROWS, PAD = 14, 80, 8
T0, OWN = 5, (24, ROWS)
FIELDS = 13
F32, BF16, I32 = jnp.float32, jnp.bfloat16, jnp.int32


def params(mebibytes):
    return pltpu.CompilerParams(vmem_limit_bytes=int(mebibytes * 1024 * 1024))


def shape(dims, dtype):
    return jax.ShapeDtypeStruct(dims, dtype)


VM = pl.BlockSpec(memory_space=pltpu.VMEM)
HB = pl.BlockSpec(memory_space=pltpu.HBM)


def roll(values, shift, axis):
    return pltpu.roll(values, shift, axis)


def tile_iotas():
    row = lax.broadcasted_iota(I32, (8, LANES), 0)
    lane = lax.broadcasted_iota(I32, (8, LANES), 1)
    return row, lane


def hops(v, before, after, ahead_t, behind_t, coefs):
    sign_t, sign_x, sign_y, sign_z = coefs
    p0, p1 = ahead_t[0] - ahead_t[2], ahead_t[1] - ahead_t[3]
    q0, q1 = behind_t[0] + behind_t[2], behind_t[1] + behind_t[3]
    along_t = (q0 + p0, q1 + p1, q0 - p0, q1 - p1)
    u0, u2 = after[0] - after[1], after[2] + after[3]
    w0, w2 = before[0] + before[1], before[2] - before[3]
    along_x = (w0 + u0, w0 - u0, u2 + w2, u2 - w2)
    along_y = (roll(v[0], 2, 0), roll(v[1], 6, 0), roll(v[2], 6, 0), roll(v[3], 2, 0))
    f, g = roll(v[0] + v[3], LANES - 1, 1), roll(v[1] - v[2], LANES - 1, 1)
    h, k = roll(v[0] - v[3], 1, 1), roll(v[1] + v[2], 1, 1)
    along_z = (f + h, k + g, k - g, f - h)
    return [
        (sign_t * along_t[s] + sign_x * along_x[s]) + (sign_y * along_y[s] + sign_z * along_z[s])
        for s in range(4)
    ]


def layer_rows(layer):
    start = 2 * PAD + 8 * layer
    return slice(start, start + 8)


def visit(field, signs, slices, tiles, put):
    lows = slices[0::2]
    length = slices[1] - slices[0]

    def body(step, carry):
        t = step + lows[0] if len(lows) == 1 else jnp.where(step < length, step + lows[0], step - length + lows[1])

        def spins_at(time, layer):
            return [field[s, time, layer_rows(layer), :] for s in range(4)]

        first = 2 * tiles[0]
        before, here = spins_at(t, first - 1), spins_at(t, first)
        for layer in range(first, 2 * tiles[1]):
            coefs = [signs[m, t, layer_rows(layer), :] for m in range(4)]
            after = spins_at(t, layer + 1)
            put(t, layer, here, hops(here, before, after, spins_at(t + 1, layer), spins_at(t - 1, layer), coefs))
            before, here = here, after
        return carry

    lax.fori_loop(0, length * len(lows), body, 0)


def chosen(plan, colour, t, layer, lane):
    block = lax.axis_index("ta") + (t + 3) // 4 + layer // 4 + 1
    return ((lane >> 2) & 1) == ((plan[colour] + block) & 1)


def half_sweep(plan, colour, target, field, source, signs, inverse, slices, tiles, lane):
    def put(t, layer, centre, sums):
        rows = layer_rows(layer)
        mask = chosen(plan, colour, t, layer, lane)
        scale = inverse[t, rows, :]
        for s in range(4):
            value = (source[s, t, rows, :] + sums[s]) * scale
            target[s, t, rows, :] = jnp.where(mask, value, centre[s])

    visit(field, signs, slices, tiles, put)


def wide_sweep(plan, colour, depth, target, field, src, signs, inverse, lane):
    done = 0
    while done <= depth:
        tiles = (2, 6) if depth == done else (1, 7) if depth - done <= 2 else (0, 8)
        last = depth if depth == done else depth - 1 if depth - done <= 2 else depth - 3
        if done == 0:
            slices = (T0 - last, T0 + LT + last)
        else:
            slices = (T0 - last, T0 - done + 1, T0 + LT + done - 1, T0 + LT + last)
        half_sweep(plan, colour, target, field, src, signs, inverse, slices, tiles, lane)
        done = last + 1


def places():
    t_odd, x_odd = lax.axis_index("ta") & 1, lax.axis_index("xyz") & 1
    return (t_odd, 1 - t_odd), (x_odd, 1 - x_odd)


def x_start(before):
    return PAD + 48 * (1 - before)


def side_rows(rows, n):
    return pl.ds(2 * rows[0] + n, rows[1], stride=2)


def column_of(data, t, before, first):
    pair = data[8 * (t // 2) : 8 * (t // 2) + 8]
    turned = roll(pair, 4, 0)
    top, bottom = (pair, turned) if t % 2 == 0 else (turned, pair)
    return jnp.where(before == 0, jnp.where(first, top, 0.0), jnp.where(first, 0.0, bottom))


def put_cross(fields, ta, tb, xa, xb, put, add_low, first):
    t_before, x_before = places()
    for data, before in ((ta, t_before[0]), (tb, t_before[1])):
        for part in range(2):
            base = T0 + LT - 8 * before + 2 * part

            def t_slice(t, carry, data=data[part], base=base):
                for c in range(fields):
                    put(c, base + t, OWN, data[fields * t + c].astype(F32))
                return carry

            lax.fori_loop(0, 2, t_slice, 0)
        near = T0 + LT - 5 * before
        for c in range(8):
            add_low(c, near, OWN, data[c // 4][2 * fields + c % 4].astype(F32))
    for data, before in ((xa, x_before[0]), (xb, x_before[1])):
        start = x_start(before)

        def x_slice(t, carry, data=data, start=start):
            for c in range(fields):
                put(c, T0 + t, (start, 16), data[fields * t + c].astype(F32))
            return carry

        lax.fori_loop(0, LT, x_slice, 0)
        where = (start + 8 * before, 8)
        for c in range(8):
            low = data[4 * fields + c].astype(F32)
            for t in range(LT):
                add_low(c, T0 + t, where, column_of(low, t, before, first))


def put_corners(fields, ca, cb, put, deep):
    t_before, x_before = places()
    for data, before in ((ca, t_before[0]), (cb, t_before[1])):
        near, step = T0 + LT - 5 * before, 1 - 2 * before
        for half in range(2):
            start = x_start(x_before[half])
            facing = (start + 8 * x_before[half], 8)
            part = slice(16 * half, 16 * half + 16)
            for c in range(fields):
                put(c, near, (start, 16), data[c, part, :].astype(F32))
                if deep:
                    put(c, near + step, (start, 16), data[fields + c, part, :].astype(F32))
                value = data[(1 + deep) * fields + c, part, :].astype(F32)
                put(c, near + (1 + deep) * step, facing, value[:8])
                put(c, near + (2 + deep) * step, facing, value[8:])
        if deep:
            for c in range(fields):
                put(c, (ET - 1) * (1 - before), OWN, data[3 * fields + c].astype(F32))


def low_part(value):
    return value - value.astype(BF16).astype(F32)


def pack_t(fields, read, t_a, t_b):
    t_before, _ = places()
    for part in range(2):

        def one_slice(t, carry, part=part):
            for c in range(fields):
                value = read(c, 2 * part + t).astype(BF16)
                t_a[part][fields * t + c] = value
                t_b[part][fields * t + c] = value
            return carry

        lax.fori_loop(0, 2, one_slice, 0)
    for c in range(8):
        for out, before in ((t_a, t_before[0]), (t_b, t_before[1])):
            out[c // 4][2 * fields + c % 4] = low_part(read(c, 3 * (1 - before))).astype(BF16)


def pack_x(fields, read, x_a, x_b, first):
    _, x_before = places()

    def one_slice(t, carry):
        for c in range(fields):
            value = read(c, t).astype(BF16)
            x_a[fields * t + c] = jnp.where(x_before[0] == 0, value[16:], value[:16])
            x_b[fields * t + c] = jnp.where(x_before[1] == 0, value[16:], value[:16])
        return carry

    lax.fori_loop(0, LT, one_slice, 0)

    def join(tops, bottoms):
        return jnp.concatenate([jnp.where(first, tops[t], bottoms[t + 1]) for t in (0, 2)], 0)

    def turn(values):
        return [roll(value, 4, 0) for value in values]

    for c in range(8):
        values = [read(c, t) for t in range(LT)]
        lows = [low_part(value[:8]) for value in values]
        highs = [low_part(value[24:]) for value in values]
        low, high = join(lows, turn(lows)), join(turn(highs), highs)
        for out, before in ((x_a, x_before[0]), (x_b, x_before[1])):
            out[4 * fields + c] = jnp.where(before == 0, high, low).astype(BF16)
        if x_a.shape[0] > 4 * fields + 8:
            lows = [value[16:24] for value in values]
            highs = [value[8:16] for value in values]
            low, high = join(lows, turn(lows)), join(turn(highs), highs)
            for out, before in ((x_a, x_before[0]), (x_b, x_before[1])):
                out[4 * fields + 8 + c] = jnp.where(before == 0, high, low).astype(BF16)


def corner_kernel(fields, deep, *refs):
    xb, xa, *beyond, ca, cb = refs
    t_before, x_before = places()
    for out, before, behind in ((ca, t_before[0], beyond[2:]), (cb, t_before[1], beyond[:2])):
        if deep:
            for c in range(fields):
                out[3 * fields + c] = jnp.where(before == 1, behind[0][c], behind[1][fields + c])
        near, step = 3 * (1 - before), 2 * before - 1

        def one_field(c, carry, out=out, near=near, step=step):
            for half, data in enumerate((xa, xb)):
                where = slice(16 * half, 16 * half + 16)
                for depth in range(1 + deep):
                    out[depth * fields + c, where, :] = data[fields * (near + depth * step) + c]
                pieces = []
                for depth in (1 + deep, 2 + deep):
                    value = data[fields * (near + depth * step) + c].astype(F32)
                    pieces.append(jnp.where(x_before[half] == 0, value[:8], value[8:]))
                out[(1 + deep) * fields + c, where, :] = jnp.concatenate(pieces, 0).astype(BF16)
            return carry

        lax.fori_loop(0, fields, one_field, 0)


def input_reader(source, mass, links):
    def read(c, t):
        if c < 8:
            return source[c, t]
        if c == 8:
            return mass[t]
        return (1.0 if c == 11 else 0.5) * (1 - 2 * links[c - 9, t]).astype(F32)

    return read


def field_writer(field):
    def put(c, t, rows, value):
        field[c // 2, t, side_rows(rows, c % 2), :] = value

    return put


def input_writer(src, signs, inverse):
    put_source = field_writer(src)

    def put(c, t, rows, value):
        if c < 8:
            put_source(c, t, rows, value)
            return
        if c == 8:
            value = 1.0 / (4.0 + value)
        for n in range(RHS):
            if c == 8:
                inverse[t, side_rows(rows, n), :] = value
            else:
                signs[c - 9, t, side_rows(rows, n), :] = value

    return put


def adder(field):
    def add_low(c, t, rows, value):
        where = side_rows(rows, c % 2)
        field[c // 2, t, where, :] = field[c // 2, t, where, :] + value

    return add_low


def load_kernel(source, mass, links, source_out, mass_out, links_out, x_a, x_b, sems):
    pairs = ((source, source_out), (mass, mass_out), (links, links_out))
    copies = [pltpu.make_async_copy(a, b, sems.at[i]) for i, (a, b) in enumerate(pairs)]
    for copy in copies:
        copy.start()
    for copy in copies:
        copy.wait()
    first = lax.broadcasted_iota(I32, (8, LANES), 0) < 4
    pack_x(FIELDS, input_reader(source_out, mass_out, links_out), x_a, x_b, first)


def share_kernel(source, mass, links, *shares):
    pack_t(FIELDS, input_reader(source, mass, links), shares[:2], shares[2:])


def cross_kernel(
    xb, xa, tb2, tb1, ta2, ta1, source, mass, links, coarse_far, src, signs, inverse, operator, coarse, sem
):
    copy = pltpu.make_async_copy(coarse_far, coarse, sem)
    copy.start()
    read, put = input_reader(source, mass, links), input_writer(src, signs, inverse)

    def own_slice(t, carry):
        for c in range(FIELDS):
            put(c, t + T0, OWN, read(c, t))
        return carry

    lax.fori_loop(0, LT, own_slice, 0)
    first = lax.broadcasted_iota(I32, (8, LANES), 0) < 4
    put_cross(FIELDS, (ta1, ta2), (tb1, tb2), xa, xb, put, adder(src), first)
    copy.wait()
    relayout(coarse, operator)


def relayout(operator, result):
    def group(kk, carry):
        def block(b, q):
            return operator[b, 4 * kk + q].astype(F32)

        for place, kinds in enumerate(((0, 5, 6), (1,), (2,), (3,), (4,), (7,), (8,))):
            pieces = []
            for q in range(4):
                piece = block(kinds[0], q)
                for b in kinds[1:]:
                    piece = piece + block(b, q)
                pieces.append(piece)
            result[place, kk] = jnp.concatenate(pieces, axis=-1)
        return carry

    lax.fori_loop(0, 6, group, 0)


def exact_sum(matrix, values, left):
    high = values.astype(BF16)
    low = (values - high.astype(F32)).astype(BF16)

    def one(part):
        pair = (matrix, part) if left else (part, matrix)
        return jnp.dot(*pair, preferred_element_type=F32)

    return one(high) + one(low)


def fill_diag(mass, diag):
    for t in range(LT):
        for n in range(RHS):
            diag[t, side_rows((0, ROWS), n), :] = 4.0 + mass[t]


def copy_own(field, first_slice, rows, out):
    def one_slice(t, carry):
        for c in range(8):
            out[c, t] = field[c // 2, t + first_slice, side_rows(rows, c % 2), :]
        return carry

    lax.fori_loop(0, LT, one_slice, 0)


def pre_kernel(
    plan_far, mass, ca, cb, src_in, signs_in, inverse_in, near_null,
    out_solution, out_rhs, out_rounded, src, signs, inverse,
    field_a, field_b, diag, resid, sums, plan, sem,
):
    del src_in, signs_in, inverse_in
    plan_copy = pltpu.make_async_copy(plan_far, plan, sem)
    plan_copy.start()
    _, lane = tile_iotas()
    put_corners(FIELDS, ca, cb, input_writer(src, signs, inverse), 0)
    plan_copy.wait()

    def first_sweep(t, carry):
        for layer in range(16):
            rows = layer_rows(layer)
            scale = jnp.where(chosen(plan, 0, t, layer, lane), inverse[t, rows, :], 0.0)
            for s in range(4):
                field_a[s, t, rows, :] = src[s, t, rows, :] * scale
        return carry

    lax.fori_loop(1, ET - 1, first_sweep, 0)
    common = (src, signs, inverse, lane)
    wide_sweep(plan, 1, 3, field_b, field_a, *common)
    wide_sweep(plan, 2, 2, field_a, field_b, *common)
    wide_sweep(plan, 3, 1, field_b, field_a, *common)

    fill_diag(mass, diag)

    def put(t, layer, centre, hop):
        rows, inner = layer_rows(layer), slice(8 * layer - 32, 8 * layer - 24)
        for s in range(4):
            value = (src[s, t, rows, :] - diag[t - T0, inner, :] * centre[s]) + hop[s]
            resid[s, t - T0, inner, :] = value.astype(BF16).astype(F32)

    visit(field_b, signs, (T0, T0 + LT), (2, 6), put)
    copy_own(field_b, T0, OWN, out_solution)
    group = 4

    def vectors(step, carry):
        totals = {}
        for s in range(4):
            for t in range(LT):
                for block in range(2):
                    low, mid, high = 16 * block, 16 * block + 8, 16 * block + 16
                    halves = [
                        (resid[s, t, side_rows((low, 8), n), :], resid[s, t, side_rows((mid, 8), n), :]) for n in range(RHS)
                    ]
                    for i in range(group):
                        vector = near_null[group * step + i, s, t, low:high, :].astype(F32)
                        for n in range(RHS):
                            term = vector[:8] * halves[n][0] + vector[8:] * halves[n][1]
                            key = (i, n, block)
                            totals[key] = term if key not in totals else totals[key] + term
        for (i, n, block), value in totals.items():
            place = 8 * (48 * n + 2 * (group * step + i) + block)
            sums[pl.ds(pl.multiple_of(place, 8), 8), :] = value
        return carry

    lax.fori_loop(0, NVEC // group, vectors, 0)
    count = 2 * NVEC * RHS
    fold = jnp.where(
        lax.broadcasted_iota(I32, (count, 8 * count), 1) >> 3 == lax.broadcasted_iota(I32, (count, 8 * count), 0), 1.0, 0.0
    ).astype(BF16)
    spread = jnp.where(
        lax.broadcasted_iota(I32, (LANES, LANES), 0) >> 2 == lax.broadcasted_iota(I32, (LANES, LANES), 1) & 31, 1.0, 0.0
    ).astype(BF16)
    rhs = exact_sum(spread, exact_sum(fold, sums[...], True), False)
    out_rhs[...] = rhs
    out_rounded[...] = rhs.astype(BF16)


def coarse_step(operator, rhs, estimate, rounded, ta, tb, xa, xb, beside, out):
    row, lane = tile_iotas()
    t_odd, x_odd = lax.axis_index("ta") & 1, lax.axis_index("xyz") & 1
    even_row = (row & 1) == 0
    for i in range(12):
        where = slice(8 * i, 8 * i + 8)
        own = rounded[where].astype(F32)
        t_first, t_second = ta[where].astype(F32), tb[where].astype(F32)
        x_first, x_second = xa[where].astype(F32), xb[where].astype(F32)
        beside[0, where] = own
        beside[1, where] = jnp.where(t_odd == 0, t_first, t_second)
        beside[2, where] = jnp.where(t_odd == 0, t_second, t_first)
        after = jnp.where(x_odd == 0, x_first, x_second)
        before = jnp.where(x_odd == 0, x_second, x_first)
        own_up, own_down = roll(own, 7, 0), roll(own, 1, 0)
        beside[3, where] = jnp.where(even_row, own_up, roll(after, 1, 0))
        beside[4, where] = jnp.where(even_row, roll(before, 7, 0), own_down)
        beside[5, where] = roll(own, LANES - 1, 1)
        beside[6, where] = roll(own, 1, 1)
    totals = [[None] * RHS for _ in range(6)]
    for b in range(7):
        near = [[beside[b, 48 * n + 8 * j : 48 * n + 8 * j + 8, :] for j in range(6)] for n in range(RHS)]
        for kk in range(6):
            for j in range(6):
                block = operator[b, kk, 8 * j : 8 * j + 8, :]
                for n in range(RHS):
                    term = block * near[n][j]
                    totals[kk][n] = term if totals[kk][n] is None else totals[kk][n] + term
    diagonal = (lane >> 5) == (row >> 1)
    for n in range(RHS):
        for kk in range(6):
            where = slice(48 * n + 8 * kk, 48 * n + 8 * kk + 8)
            value = totals[kk][n]
            value = value + roll(value, 4, 0)
            value = value + roll(value, 2, 0)
            value = jnp.where(diagonal, value, 0.0)
            value = value + roll(value, 64, 1)
            value = value + roll(value, 32, 1)
            out[where] = estimate[where] + (rhs[where] - value)


def coarse_kernel(operator, rhs, estimate, rounded, ta, tb, xa, xb, out, out_rounded, beside):
    coarse_step(operator, rhs, estimate, rounded, ta, tb, xa, xb, beside, out)
    out_rounded[...] = out[...].astype(BF16)


def prolong_kernel(
    operator, rhs, estimate, rounded, ta, tb, xa, xb, near_null, solution,
    out, x_a, x_b,
    beside, final, spread_rows,
):
    coarse_step(operator, rhs, estimate, rounded, ta, tb, xa, xb, beside, final)
    widen = jnp.where(
        lax.broadcasted_iota(I32, (LANES, LANES), 0) == lax.broadcasted_iota(I32, (LANES, LANES), 1) >> 2, 1.0, 0.0
    ).astype(BF16)
    wide = jnp.dot(final[...].astype(BF16), widen, preferred_element_type=F32)
    for i in range(2 * NVEC * RHS):
        spread_rows[i] = jnp.broadcast_to(wide[i : i + 1, :], (8, LANES))

    def body(step, carry):
        s, t = step // LT, step % LT
        for block in range(2):
            low, mid, high = 16 * block, 16 * block + 8, 16 * block + 16
            totals = [None] * RHS
            for k in range(NVEC):
                vector = near_null[k, s, t, low:high, :].astype(F32)
                for n in range(RHS):
                    weight = spread_rows[48 * n + 2 * k + block]
                    term = (vector[:8] * weight, vector[8:] * weight)
                    old = totals[n]
                    totals[n] = term if old is None else (old[0] + term[0], old[1] + term[1])
            for n in range(RHS):
                for part, span in enumerate((slice(low, mid), slice(mid, high))):
                    out[2 * s + n, t, span, :] = solution[2 * s + n, t, span, :] + totals[n][part]
        return carry

    lax.fori_loop(0, 4 * LT, body, 0)
    first = lax.broadcasted_iota(I32, (8, LANES), 0) < 4
    pack_x(8, lambda c, t: out[c, t], x_a, x_b, first)


def share_field_kernel(solution, *shares):
    pack_t(8, lambda c, t: solution[c, t], shares[:2], shares[2:])


def field_kernel(xb, xa, tb2, tb1, ta2, ta1, solution, field):
    put = field_writer(field)

    def own_slice(t, carry):
        for c in range(8):
            put(c, t + T0, OWN, solution[c, t])
        return carry

    lax.fori_loop(0, LT, own_slice, 0)
    first = lax.broadcasted_iota(I32, (8, LANES), 0) < 4
    put_cross(8, (ta1, ta2), (tb1, tb2), xa, xb, put, adder(field), first)
    _, x_before = places()
    for data, before in ((xa, x_before[0]), (xb, x_before[1])):
        where = ((EROWS - 8) * (1 - before), 8)
        for c in range(8):
            layer = data[40 + c].astype(F32)
            for t in range(LT):
                put(c, T0 + t, where, column_of(layer, t, before, first))


def post_kernel(
    plan_far, mass, src, signs, inverse, field_in, ca, cb, out, residual, field_a, field_b, diag, resid, plan, sem
):
    del field_in
    plan_copy = pltpu.make_async_copy(plan_far, plan, sem)
    plan_copy.start()
    row, lane = tile_iotas()

    put_corners(8, ca, cb, field_writer(field_a), 1)
    fill_diag(mass, diag)
    plan_copy.wait()
    common = (src, signs, inverse, lane)
    wide_sweep(plan, 4, 4, field_b, field_a, *common)
    wide_sweep(plan, 5, 3, field_a, field_b, *common)
    wide_sweep(plan, 6, 2, field_b, field_a, *common)
    wide_sweep(plan, 7, 1, field_a, field_b, *common)

    def put(t, layer, centre, hop):
        rows, inner = layer_rows(layer), slice(8 * layer - 32, 8 * layer - 24)
        for s in range(4):
            resid[s, t - T0, inner, :] = (src[s, t, rows, :] - diag[t - T0, inner, :] * centre[s]) + hop[s]

    visit(field_a, signs, (T0, T0 + LT), (2, 6), put)
    copy_own(field_a, T0, OWN, out)
    copy_own(resid, 0, (0, ROWS), residual)


def call(kernel, mebibytes, outs, scratch, *args, aliases=(), far=(), cost=None):
    scratch = [item if not isinstance(item, tuple) else pltpu.VMEM(item, F32) for item in scratch]
    specs = [HB if i in far else VM for i in range(len(args))]
    return pl.pallas_call(
        kernel,
        out_shape=outs,
        in_specs=specs,
        out_specs=[VM] * len(outs),
        scratch_shapes=scratch,
        input_output_aliases=dict(aliases),
        compiler_params=params(mebibytes),
        cost_estimate=cost and pl.CostEstimate(flops=cost, bytes_accessed=cost, transcendentals=0),
    )(*args)


def swap(values, axis, odd_pairs):
    devices = lax.axis_size(axis)
    if odd_pairs:
        pairs = [(i, (i + 1) % devices if i % 2 else (i - 1) % devices) for i in range(devices)]
    else:
        pairs = [(i, i ^ 1) for i in range(devices)]
    return lax.ppermute(values, axis, pairs)


def swap_four(t_first, t_second, x_first, x_second):
    xb = swap(x_second, "xyz", True)
    xa = swap(x_first, "xyz", False)
    tb = swap(t_second, "ta", True)
    ta = swap(t_first, "ta", False)
    return ta, tb, xa, xb


def slabs(count, rows):
    return shape((count, rows, LANES), BF16)


def swap_six(ta1, ta2, tb1, tb2, x_first, x_second):
    xb = swap(x_second, "xyz", True)
    xa = swap(x_first, "xyz", False)
    second = [swap(part, "ta", True) for part in (tb1, tb2)]
    return *(swap(part, "ta", False) for part in (ta1, ta2)), *second, xa, xb


def corners_of(fields, deep, *near):
    kernel = functools.partial(corner_kernel, fields, deep)
    *t_parts, xa, xb = near
    beyond = t_parts if deep else ()
    ca, cb = call(kernel, 4, [slabs((2 + 2 * deep) * fields, ROWS)] * 2, [], xb, xa, *beyond)
    cb = swap(cb, "ta", True)
    return swap(ca, "ta", False), cb


def per_device(source, mass, links, near_null, coarse_op, plan):
    out_shape = source.shape
    source = source.reshape(8, LT, ROWS, LANES)
    mass = mass.reshape(LT, ROWS, LANES)
    links = links.reshape(4, LT, ROWS, LANES)
    near_null = near_null.reshape(NVEC, 4, LT, ROWS, LANES)
    coarse_op = coarse_op.reshape(9, NVEC, 2 * NVEC, 32)
    count = 2 * NVEC * RHS
    field, own, ext = (8, LT, ROWS, LANES), (4, LT, 2 * ROWS, LANES), (4, ET, 2 * EROWS, LANES)
    inputs = [shape(ext, F32), shape(ext, F32), shape(ext[1:], F32)]

    plan = pltpu.with_memory_space_constraint(plan, pltpu.HBM)
    source, mass, links, x_a, x_b = call(
        load_kernel,
        8,
        [shape(field, F32), shape(field[1:], F32), shape((4, *field[1:]), I32)] + [slabs(4 * FIELDS + 8, 16)] * 2,
        [pltpu.SemaphoreType.DMA((3,))],
        *(pltpu.with_memory_space_constraint(value, pltpu.HBM) for value in (source, mass, links)),
        far=(0, 1, 2),
    )
    shares = call(share_kernel, 6, [slabs(2 * FIELDS + 4, ROWS)] * 4, [], source, mass, links, cost=1 << 22)
    near = swap_six(*shares, x_a, x_b)
    corners = corners_of(FIELDS, 0, *near)
    coarse_op = pltpu.with_memory_space_constraint(coarse_op, pltpu.HBM)
    src, signs, inverse, operator = call(
        cross_kernel,
        24,
        inputs + [shape((7, 6, 2 * NVEC, LANES), F32)],
        [pltpu.VMEM(coarse_op.shape, BF16), pltpu.SemaphoreType.DMA],
        *near[::-1], source, mass, links, coarse_op,
        far=(9,),
        cost=1 << 22,
    )
    solution, rhs, rounded, src, signs, inverse = call(
        pre_kernel,
        36,
        [shape(field, F32), shape((count, LANES), F32), shape((count, LANES), BF16)] + inputs,
        [ext, ext, (LT, 2 * ROWS, LANES), own, (8 * count, LANES), pltpu.SMEM((SWEEPS,), I32), pltpu.SemaphoreType.DMA],
        plan, mass, *corners, src, signs, inverse, near_null,
        aliases=((4, 3), (5, 4), (6, 5)),
        far=(0,),
    )
    estimate = rhs
    beside = (7, count, LANES)
    for turn in range(1, KC):
        near = swap_four(rounded, rounded, rounded, rounded)
        given = (operator, rhs, estimate, rounded, *near)
        if turn < KC - 1:
            outs = [shape((count, LANES), F32), shape((count, LANES), BF16)]
            estimate, rounded = call(coarse_kernel, 6, outs, [beside], *given)
    solution, x_a, x_b = call(
        prolong_kernel,
        12,
        [shape(field, F32)] + [slabs(48, 16)] * 2,
        [beside, (count, LANES), (count, 8, LANES)],
        *given, near_null, solution,
    )
    shares = call(share_field_kernel, 4, [slabs(20, ROWS)] * 4, [], solution, cost=1 << 22)
    near = swap_six(*shares, x_a, x_b)
    corners = corners_of(8, 1, *near)
    (grown,) = call(field_kernel, 10, [shape(ext, F32)], [], *near[::-1], solution, cost=1 << 22)
    solution, residual, _ = call(
        post_kernel,
        28,
        [shape(field, F32)] * 2 + [shape(ext, F32)],
        [ext, (LT, 2 * ROWS, LANES), own, pltpu.SMEM((SWEEPS,), I32), pltpu.SemaphoreType.DMA],
        plan, mass, src, signs, inverse, grown, *corners,
        aliases=((5, 2),),
        far=(0,),
    )
    return solution.reshape(out_shape), residual.reshape(out_shape)


def solution(mesh):
    return jax.shard_map(
        per_device,
        mesh=mesh,
        in_specs=(
            P(None, None, "ta", "xyz", None, None),
            P("ta", "xyz", None, None),
            P(None, "ta", "xyz", None, None),
            P(None, None, "ta", "xyz", None, None),
            P(None, None, None, "ta", "xyz", None, None),
            P(),
        ),
        out_specs=(P(None, None, "ta", "xyz", None, None), P(None, None, "ta", "xyz", None, None)),
        check_vma=False,
    )
```

```python
import functools

import jax
import jax.numpy as jnp
from jax import lax
from jax.experimental import pallas as pl
from jax.experimental.pallas import tpu as pltpu
from jax.sharding import PartitionSpec as P

LT, ROWS, LANES = 4, 32, 128
NVEC, RHS, KC, SWEEPS = 24, 2, 6, 8
ET, EROWS, PAD = 14, 80, 8
T0, OWN = 5, (24, ROWS)
FIELDS = 13
F32, BF16, I32 = jnp.float32, jnp.bfloat16, jnp.int32


def params(mebibytes):
    return pltpu.CompilerParams(vmem_limit_bytes=int(mebibytes * 1024 * 1024))


def shape(dims, dtype):
    return jax.ShapeDtypeStruct(dims, dtype)


VM = pl.BlockSpec(memory_space=pltpu.VMEM)
HB = pl.BlockSpec(memory_space=pltpu.HBM)


def roll(values, shift, axis):
    return pltpu.roll(values, shift, axis)


def tile_iotas():
    row = lax.broadcasted_iota(I32, (8, LANES), 0)
    lane = lax.broadcasted_iota(I32, (8, LANES), 1)
    return row, lane


def turns(v):
    along_y = (roll(v[0], 2, 0), roll(v[1], 6, 0), roll(v[2], 6, 0), roll(v[3], 2, 0))
    f, g = roll(v[0] + v[3], LANES - 1, 1), roll(v[1] - v[2], LANES - 1, 1)
    h, k = roll(v[0] - v[3], 1, 1), roll(v[1] + v[2], 1, 1)
    return along_y, (f, g, h, k)


def hops(turned, before, after, ahead_t, behind_t, coefs):
    sign_t, sign_x, sign_y, sign_z = coefs
    p0, p1 = ahead_t[0] - ahead_t[2], ahead_t[1] - ahead_t[3]
    q0, q1 = behind_t[0] + behind_t[2], behind_t[1] + behind_t[3]
    along_t = (q0 + p0, q1 + p1, q0 - p0, q1 - p1)
    u0, u2 = after[0] - after[1], after[2] + after[3]
    w0, w2 = before[0] + before[1], before[2] - before[3]
    along_x = (w0 + u0, w0 - u0, u2 + w2, u2 - w2)
    along_y, (f, g, h, k) = turned
    along_z = (f + h, k + g, k - g, f - h)
    return [
        (sign_t * along_t[s] + sign_x * along_x[s]) + (sign_y * along_y[s] + sign_z * along_z[s])
        for s in range(4)
    ]


def layer_rows(layer):
    start = 2 * PAD + 8 * layer
    return slice(start, start + 8)


def visit(field, signs, slices, tiles, put):
    lows = slices[0::2]
    length = slices[1] - slices[0]

    def spins_at(time, layer):
        return [field[s, time, layer_rows(layer), :] for s in range(4)]

    def layers_of(t, first, last):
        spins, turned = {first - 1: spins_at(t, first - 1)}, {}

        def prepare(layer):
            if layer <= last:
                spins[layer] = spins_at(t, layer)
            if layer < last:
                turned[layer] = turns(spins[layer])

        for layer in range(first, first + 2):
            prepare(layer)
        for layer in range(first, last):
            prepare(layer + 2)
            coefs = [signs[m, t, layer_rows(layer), :] for m in range(4)]
            sums = hops(
                turned[layer], spins[layer - 1], spins[layer + 1], spins_at(t + 1, layer), spins_at(t - 1, layer), coefs
            )
            put(t, layer, spins[layer], sums)

    def body(step, carry):
        t = step + lows[0] if len(lows) == 1 else jnp.where(step < length, step + lows[0], step - length + lows[1])
        for low, high in zip(tiles[0::2], tiles[1::2]):
            layers_of(t, 2 * low, 2 * high)
        return carry

    lax.fori_loop(0, length * len(lows), body, 0, unroll=2)


def chosen(plan, colour, t, layer, lane):
    block = lax.axis_index("ta") + (t + 3) // 4 + layer // 4 + 1
    return ((lane >> 2) & 1) == ((plan[colour] + block) & 1)


def half_sweep(plan, colour, target, field, source, signs, inverse, slices, tiles, lane):
    def put(t, layer, centre, sums):
        rows = layer_rows(layer)
        mask = chosen(plan, colour, t, layer, lane)
        scale = inverse[t, rows, :]
        for s in range(4):
            value = (source[s, t, rows, :] + sums[s]) * scale
            target[s, t, rows, :] = jnp.where(mask, value, centre[s])

    visit(field, signs, slices, tiles, put)


EARLY = (((6, 8), (0, 8)), ((5, 6, 8, 9), (2, 6)), ((2, 5, 9, 12), (3, 5)))
LATE = {
    3: (((5, 6, 8, 9), (0, 2, 6, 8)), ((3, 5, 9, 11), (1, 3, 5, 7)), ((2, 3, 11, 12), (2, 3, 5, 6))),
    4: (
        ((5, 6, 8, 9), (0, 2, 6, 8)),
        ((4, 5, 9, 10), (0, 3, 5, 8)),
        ((2, 4, 10, 12), (1, 3, 5, 7)),
        ((1, 2, 12, 13), (2, 6)),
    ),
}


def part_sweep(plan, colour, parts, target, field, src, signs, inverse, lane):
    for slices, tiles in parts:
        half_sweep(plan, colour, target, field, src, signs, inverse, slices, tiles, lane)


def first_values(plan, target, src, inverse, lane, low, high, layers):
    def one_slice(t, carry):
        for layer in layers:
            rows = layer_rows(layer)
            scale = jnp.where(chosen(plan, 0, t, layer, lane), inverse[t, rows, :], 0.0)
            for s in range(4):
                target[s, t, rows, :] = src[s, t, rows, :] * scale
        return carry

    lax.fori_loop(low, high, one_slice, 0)


OWN_LAYERS, HALO_LAYERS = tuple(range(4, 12)), (0, 1, 2, 3, 12, 13, 14, 15)


def wide_sweep(plan, colour, depth, target, field, src, signs, inverse, lane):
    done = 0
    while done <= depth:
        tiles = (2, 6) if depth == done else (1, 7) if depth - done <= 2 else (0, 8)
        last = depth if depth == done else depth - 1 if depth - done <= 2 else depth - 3
        if done == 0:
            slices = (T0 - last, T0 + LT + last)
        else:
            slices = (T0 - last, T0 - done + 1, T0 + LT + done - 1, T0 + LT + last)
        half_sweep(plan, colour, target, field, src, signs, inverse, slices, tiles, lane)
        done = last + 1


def places():
    t_odd, x_odd = lax.axis_index("ta") & 1, lax.axis_index("xyz") & 1
    return (t_odd, 1 - t_odd), (x_odd, 1 - x_odd)


def x_start(before):
    return PAD + 48 * (1 - before)


def side_rows(rows, n):
    return pl.ds(2 * rows[0] + n, rows[1], stride=2)


def column_of(data, t, before, first):
    pair = data[8 * (t // 2) : 8 * (t // 2) + 8]
    turned = roll(pair, 4, 0)
    top, bottom = (pair, turned) if t % 2 == 0 else (turned, pair)
    return jnp.where(before == 0, jnp.where(first, top, 0.0), jnp.where(first, 0.0, bottom))


def put_cross(fields, ta, tb, xa, xb, put, add_low, first):
    t_before, x_before = places()
    for data, before in ((ta, t_before[0]), (tb, t_before[1])):
        for part in range(2):
            base = T0 + LT - 8 * before + 2 * part

            def t_slice(t, carry, data=data[part], base=base):
                for c in range(fields):
                    put(c, base + t, OWN, data[fields * t + c].astype(F32))
                return carry

            lax.fori_loop(0, 2, t_slice, 0)
        near = T0 + LT - 5 * before
        for c in range(8):
            add_low(c, near, OWN, data[c // 4][2 * fields + c % 4].astype(F32))
    for data, before in ((xa, x_before[0]), (xb, x_before[1])):
        start = x_start(before)

        def x_slice(t, carry, data=data, start=start):
            for c in range(fields):
                put(c, T0 + t, (start, 16), data[fields * t + c].astype(F32))
            return carry

        lax.fori_loop(0, LT, x_slice, 0)
        where = (start + 8 * before, 8)
        for c in range(8):
            low = data[4 * fields + c].astype(F32)
            for t in range(LT):
                add_low(c, T0 + t, where, column_of(low, t, before, first))


def put_corners(fields, ca, cb, put, deep):
    t_before, x_before = places()
    for data, before in ((ca, t_before[0]), (cb, t_before[1])):
        near, step = T0 + LT - 5 * before, 1 - 2 * before
        for half in range(2):
            start = x_start(x_before[half])
            facing = (start + 8 * x_before[half], 8)
            part = slice(16 * half, 16 * half + 16)
            for c in range(fields):
                put(c, near, (start, 16), data[c, part, :].astype(F32))
                if deep:
                    put(c, near + step, (start, 16), data[fields + c, part, :].astype(F32))
                value = data[(1 + deep) * fields + c, part, :].astype(F32)
                put(c, near + (1 + deep) * step, facing, value[:8])
                put(c, near + (2 + deep) * step, facing, value[8:])
        if deep:
            for c in range(fields):
                put(c, (ET - 1) * (1 - before), OWN, data[3 * fields + c].astype(F32))


def low_part(value):
    return value - value.astype(BF16).astype(F32)


def pack_t(fields, read, t_a, t_b):
    t_before, _ = places()
    for part in range(2):

        def one_slice(t, carry, part=part):
            for c in range(fields):
                value = read(c, 2 * part + t).astype(BF16)
                t_a[part][fields * t + c] = value
                t_b[part][fields * t + c] = value
            return carry

        lax.fori_loop(0, 2, one_slice, 0)
    for c in range(8):
        for out, before in ((t_a, t_before[0]), (t_b, t_before[1])):
            out[c // 4][2 * fields + c % 4] = low_part(read(c, 3 * (1 - before))).astype(BF16)


def pack_x(fields, read, x_a, x_b, first):
    _, x_before = places()

    def one_slice(t, carry):
        for c in range(fields):
            value = read(c, t).astype(BF16)
            x_a[fields * t + c] = jnp.where(x_before[0] == 0, value[16:], value[:16])
            x_b[fields * t + c] = jnp.where(x_before[1] == 0, value[16:], value[:16])
        return carry

    lax.fori_loop(0, LT, one_slice, 0)

    def join(tops, bottoms):
        return jnp.concatenate([jnp.where(first, tops[t], bottoms[t + 1]) for t in (0, 2)], 0)

    def turn(values):
        return [roll(value, 4, 0) for value in values]

    for c in range(8):
        values = [read(c, t) for t in range(LT)]
        lows = [low_part(value[:8]) for value in values]
        highs = [low_part(value[24:]) for value in values]
        low, high = join(lows, turn(lows)), join(turn(highs), highs)
        for out, before in ((x_a, x_before[0]), (x_b, x_before[1])):
            out[4 * fields + c] = jnp.where(before == 0, high, low).astype(BF16)
        if x_a.shape[0] > 4 * fields + 8:
            lows = [value[16:24] for value in values]
            highs = [value[8:16] for value in values]
            low, high = join(lows, turn(lows)), join(turn(highs), highs)
            for out, before in ((x_a, x_before[0]), (x_b, x_before[1])):
                out[4 * fields + 8 + c] = jnp.where(before == 0, high, low).astype(BF16)


def corner_kernel(fields, deep, *refs):
    xb, xa, *beyond, ca, cb = refs
    t_before, x_before = places()
    for out, before, behind in ((ca, t_before[0], beyond[2:]), (cb, t_before[1], beyond[:2])):
        if deep:
            for c in range(fields):
                out[3 * fields + c] = jnp.where(before == 1, behind[0][c], behind[1][fields + c])
        near, step = 3 * (1 - before), 2 * before - 1

        def one_field(c, carry, out=out, near=near, step=step):
            for half, data in enumerate((xa, xb)):
                where = slice(16 * half, 16 * half + 16)
                for depth in range(1 + deep):
                    out[depth * fields + c, where, :] = data[fields * (near + depth * step) + c]
                pieces = []
                for depth in (1 + deep, 2 + deep):
                    value = data[fields * (near + depth * step) + c].astype(F32)
                    pieces.append(jnp.where(x_before[half] == 0, value[:8], value[8:]))
                out[(1 + deep) * fields + c, where, :] = jnp.concatenate(pieces, 0).astype(BF16)
            return carry

        lax.fori_loop(0, fields, one_field, 0)


def input_reader(source, mass, links):
    def read(c, t):
        if c < 8:
            return source[c, t]
        if c == 8:
            return mass[t]
        return (1.0 if c == 11 else 0.5) * (1 - 2 * links[c - 9, t]).astype(F32)

    return read


def field_writer(field):
    def put(c, t, rows, value):
        field[c // 2, t, side_rows(rows, c % 2), :] = value

    return put


def input_writer(src, signs, inverse):
    put_source = field_writer(src)

    def put(c, t, rows, value):
        if c < 8:
            put_source(c, t, rows, value)
            return
        if c == 8:
            value = 1.0 / (4.0 + value)
        for n in range(RHS):
            if c == 8:
                inverse[t, side_rows(rows, n), :] = value
            else:
                signs[c - 9, t, side_rows(rows, n), :] = value

    return put


def adder(field):
    def add_low(c, t, rows, value):
        where = side_rows(rows, c % 2)
        field[c // 2, t, where, :] = field[c // 2, t, where, :] + value

    return add_low


def load_kernel(source, mass, links, source_out, mass_out, links_out, x_a, x_b, sems):
    pairs = ((source, source_out), (mass, mass_out), (links, links_out))
    copies = [pltpu.make_async_copy(a, b, sems.at[i]) for i, (a, b) in enumerate(pairs)]
    for copy in copies:
        copy.start()
    for copy in copies:
        copy.wait()
    first = lax.broadcasted_iota(I32, (8, LANES), 0) < 4
    pack_x(FIELDS, input_reader(source_out, mass_out, links_out), x_a, x_b, first)


def share_kernel(source, mass, links, *shares):
    pack_t(FIELDS, input_reader(source, mass, links), shares[:2], shares[2:])


def cross_kernel(
    xb, xa, tb2, tb1, ta2, ta1, source, mass, links, coarse_far, plan_far,
    src, signs, inverse, field_a, field_b, operator,
    coarse, plan, sems,
):
    plan_copy = pltpu.make_async_copy(plan_far, plan, sems.at[0])
    plan_copy.start()
    copy = pltpu.make_async_copy(coarse_far, coarse, sems.at[1])
    copy.start()
    read, put = input_reader(source, mass, links), input_writer(src, signs, inverse)

    def own_slice(t, carry):
        for c in range(FIELDS):
            put(c, t + T0, OWN, read(c, t))
        return carry

    lax.fori_loop(0, LT, own_slice, 0)
    first = lax.broadcasted_iota(I32, (8, LANES), 0) < 4
    put_cross(FIELDS, (ta1, ta2), (tb1, tb2), xa, xb, put, adder(src), first)
    plan_copy.wait()
    _, lane = tile_iotas()
    first_values(plan, field_a, src, inverse, lane, 1, ET - 1, OWN_LAYERS)
    first_values(plan, field_a, src, inverse, lane, T0, T0 + LT, HALO_LAYERS)
    part_sweep(plan, 1, EARLY, field_b, field_a, src, signs, inverse, lane)
    copy.wait()
    relayout(coarse, operator)


def relayout(operator, result):
    def group(kk, carry):
        def block(b, q):
            return operator[b, 4 * kk + q].astype(F32)

        for place, kinds in enumerate(((0, 5, 6), (1,), (2,), (3,), (4,), (7,), (8,))):
            pieces = []
            for q in range(4):
                piece = block(kinds[0], q)
                for b in kinds[1:]:
                    piece = piece + block(b, q)
                pieces.append(piece)
            result[place, kk] = jnp.concatenate(pieces, axis=-1)
        return carry

    lax.fori_loop(0, 6, group, 0)


def exact_sum(matrix, values, left):
    high = values.astype(BF16)
    low = (values - high.astype(F32)).astype(BF16)

    def one(part):
        pair = (matrix, part) if left else (part, matrix)
        return jnp.dot(*pair, preferred_element_type=F32)

    return one(high) + one(low)


def fill_diag(mass, diag):
    for t in range(LT):
        for n in range(RHS):
            diag[t, side_rows((0, ROWS), n), :] = 4.0 + mass[t]


def copy_own(field, first_slice, rows, out):
    def one_slice(t, carry):
        for c in range(8):
            out[c, t] = field[c // 2, t + first_slice, side_rows(rows, c % 2), :]
        return carry

    lax.fori_loop(0, LT, one_slice, 0)


def pre_kernel(
    plan_far, mass, ca, cb, src_in, signs_in, inverse_in, field_a_in, field_b_in, near_null,
    out_solution, out_rhs, out_rounded, src, signs, inverse, field_a, field_b,
    diag, resid, sums, plan, sem,
):
    del src_in, signs_in, inverse_in, field_a_in, field_b_in
    plan_copy = pltpu.make_async_copy(plan_far, plan, sem)
    plan_copy.start()
    _, lane = tile_iotas()
    put_corners(FIELDS, ca, cb, input_writer(src, signs, inverse), 0)
    plan_copy.wait()

    first_values(plan, field_a, src, inverse, lane, 1, T0, HALO_LAYERS)
    first_values(plan, field_a, src, inverse, lane, T0 + LT, ET - 1, HALO_LAYERS)
    common = (src, signs, inverse, lane)
    part_sweep(plan, 1, LATE[3], field_b, field_a, *common)
    wide_sweep(plan, 2, 2, field_a, field_b, *common)
    wide_sweep(plan, 3, 1, field_b, field_a, *common)

    fill_diag(mass, diag)

    def put(t, layer, centre, hop):
        rows, inner = layer_rows(layer), slice(8 * layer - 32, 8 * layer - 24)
        for s in range(4):
            value = (src[s, t, rows, :] - diag[t - T0, inner, :] * centre[s]) + hop[s]
            resid[s, t - T0, inner, :] = value.astype(BF16).astype(F32)

    visit(field_b, signs, (T0, T0 + LT), (2, 6), put)
    copy_own(field_b, T0, OWN, out_solution)
    group = 4

    def vectors(step, carry):
        totals = {}
        for s in range(4):
            for t in range(LT):
                for block in range(2):
                    low, mid, high = 16 * block, 16 * block + 8, 16 * block + 16
                    halves = [
                        (resid[s, t, side_rows((low, 8), n), :], resid[s, t, side_rows((mid, 8), n), :]) for n in range(RHS)
                    ]
                    for i in range(group):
                        vector = near_null[group * step + i, s, t, low:high, :].astype(F32)
                        for n in range(RHS):
                            term = vector[:8] * halves[n][0] + vector[8:] * halves[n][1]
                            key = (i, n, block)
                            totals[key] = term if key not in totals else totals[key] + term
        for (i, n, block), value in totals.items():
            place = 8 * (48 * n + 2 * (group * step + i) + block)
            sums[pl.ds(pl.multiple_of(place, 8), 8), :] = value
        return carry

    lax.fori_loop(0, NVEC // group, vectors, 0)
    count = 2 * NVEC * RHS
    fold = jnp.where(
        lax.broadcasted_iota(I32, (count, 8 * count), 1) >> 3 == lax.broadcasted_iota(I32, (count, 8 * count), 0), 1.0, 0.0
    ).astype(BF16)
    spread = jnp.where(
        lax.broadcasted_iota(I32, (LANES, LANES), 0) >> 2 == lax.broadcasted_iota(I32, (LANES, LANES), 1) & 31, 1.0, 0.0
    ).astype(BF16)
    rhs = exact_sum(spread, exact_sum(fold, sums[...], True), False)
    out_rhs[...] = rhs
    out_rounded[...] = rhs.astype(BF16)


def coarse_step(operator, rhs, estimate, rounded, ta, tb, xa, xb, beside, out):
    row, lane = tile_iotas()
    t_odd, x_odd = lax.axis_index("ta") & 1, lax.axis_index("xyz") & 1
    even_row = (row & 1) == 0
    for i in range(12):
        where = slice(8 * i, 8 * i + 8)
        own = rounded[where].astype(F32)
        t_first, t_second = ta[where].astype(F32), tb[where].astype(F32)
        x_first, x_second = xa[where].astype(F32), xb[where].astype(F32)
        beside[0, where] = own
        beside[1, where] = jnp.where(t_odd == 0, t_first, t_second)
        beside[2, where] = jnp.where(t_odd == 0, t_second, t_first)
        after = jnp.where(x_odd == 0, x_first, x_second)
        before = jnp.where(x_odd == 0, x_second, x_first)
        own_up, own_down = roll(own, 7, 0), roll(own, 1, 0)
        beside[3, where] = jnp.where(even_row, own_up, roll(after, 1, 0))
        beside[4, where] = jnp.where(even_row, roll(before, 7, 0), own_down)
        beside[5, where] = roll(own, LANES - 1, 1)
        beside[6, where] = roll(own, 1, 1)
    totals = [[None] * RHS for _ in range(6)]
    for b in range(7):
        near = [[beside[b, 48 * n + 8 * j : 48 * n + 8 * j + 8, :] for j in range(6)] for n in range(RHS)]
        for kk in range(6):
            for j in range(6):
                block = operator[b, kk, 8 * j : 8 * j + 8, :]
                for n in range(RHS):
                    term = block * near[n][j]
                    totals[kk][n] = term if totals[kk][n] is None else totals[kk][n] + term
    diagonal = (lane >> 5) == (row >> 1)
    for n in range(RHS):
        for kk in range(6):
            where = slice(48 * n + 8 * kk, 48 * n + 8 * kk + 8)
            value = totals[kk][n]
            value = value + roll(value, 4, 0)
            value = value + roll(value, 2, 0)
            value = jnp.where(diagonal, value, 0.0)
            value = value + roll(value, 64, 1)
            value = value + roll(value, 32, 1)
            out[where] = estimate[where] + (rhs[where] - value)


def coarse_kernel(operator, rhs, estimate, rounded, ta, tb, xa, xb, out, out_rounded, beside):
    coarse_step(operator, rhs, estimate, rounded, ta, tb, xa, xb, beside, out)
    out_rounded[...] = out[...].astype(BF16)


def prolong_kernel(
    operator, rhs, estimate, rounded, ta, tb, xa, xb, near_null, solution,
    out, x_a, x_b,
    beside, final, spread_rows,
):
    coarse_step(operator, rhs, estimate, rounded, ta, tb, xa, xb, beside, final)
    widen = jnp.where(
        lax.broadcasted_iota(I32, (LANES, LANES), 0) == lax.broadcasted_iota(I32, (LANES, LANES), 1) >> 2, 1.0, 0.0
    ).astype(BF16)
    wide = jnp.dot(final[...].astype(BF16), widen, preferred_element_type=F32)
    for i in range(2 * NVEC * RHS):
        spread_rows[i] = jnp.broadcast_to(wide[i : i + 1, :], (8, LANES))

    def body(step, carry):
        s, t = step // LT, step % LT
        for block in range(2):
            low, mid, high = 16 * block, 16 * block + 8, 16 * block + 16
            totals = [None] * RHS
            for k in range(NVEC):
                vector = near_null[k, s, t, low:high, :].astype(F32)
                for n in range(RHS):
                    weight = spread_rows[48 * n + 2 * k + block]
                    term = (vector[:8] * weight, vector[8:] * weight)
                    old = totals[n]
                    totals[n] = term if old is None else (old[0] + term[0], old[1] + term[1])
            for n in range(RHS):
                for part, span in enumerate((slice(low, mid), slice(mid, high))):
                    out[2 * s + n, t, span, :] = solution[2 * s + n, t, span, :] + totals[n][part]
        return carry

    lax.fori_loop(0, 4 * LT, body, 0)
    first = lax.broadcasted_iota(I32, (8, LANES), 0) < 4
    pack_x(8, lambda c, t: out[c, t], x_a, x_b, first)


def share_field_kernel(solution, *shares):
    pack_t(8, lambda c, t: solution[c, t], shares[:2], shares[2:])


def field_kernel(
    xb, xa, tb2, tb1, ta2, ta1, solution, src, signs, inverse, plan_far, field, swept, plan, sem
):
    plan_copy = pltpu.make_async_copy(plan_far, plan, sem)
    plan_copy.start()
    put = field_writer(field)

    def own_slice(t, carry):
        for c in range(8):
            put(c, t + T0, OWN, solution[c, t])
        return carry

    lax.fori_loop(0, LT, own_slice, 0)
    first = lax.broadcasted_iota(I32, (8, LANES), 0) < 4
    put_cross(8, (ta1, ta2), (tb1, tb2), xa, xb, put, adder(field), first)
    _, x_before = places()
    for data, before in ((xa, x_before[0]), (xb, x_before[1])):
        where = ((EROWS - 8) * (1 - before), 8)
        for c in range(8):
            layer = data[40 + c].astype(F32)
            for t in range(LT):
                put(c, T0 + t, where, column_of(layer, t, before, first))
    plan_copy.wait()
    _, lane = tile_iotas()
    part_sweep(plan, 4, EARLY, swept, field, src, signs, inverse, lane)


def post_kernel(
    plan_far, mass, src, signs, inverse, field_a_in, field_b_in, ca, cb,
    out, residual, field_a, field_b,
    diag, resid, plan, sem,
):
    del field_a_in, field_b_in
    plan_copy = pltpu.make_async_copy(plan_far, plan, sem)
    plan_copy.start()
    row, lane = tile_iotas()

    put_corners(8, ca, cb, field_writer(field_a), 1)
    fill_diag(mass, diag)
    plan_copy.wait()
    common = (src, signs, inverse, lane)
    part_sweep(plan, 4, LATE[4], field_b, field_a, *common)
    wide_sweep(plan, 5, 3, field_a, field_b, *common)
    wide_sweep(plan, 6, 2, field_b, field_a, *common)
    wide_sweep(plan, 7, 1, field_a, field_b, *common)

    def put(t, layer, centre, hop):
        rows, inner = layer_rows(layer), slice(8 * layer - 32, 8 * layer - 24)
        for s in range(4):
            resid[s, t - T0, inner, :] = (src[s, t, rows, :] - diag[t - T0, inner, :] * centre[s]) + hop[s]

    visit(field_a, signs, (T0, T0 + LT), (2, 6), put)
    copy_own(field_a, T0, OWN, out)
    copy_own(resid, 0, (0, ROWS), residual)


def call(kernel, mebibytes, outs, scratch, *args, aliases=(), far=(), cost=None):
    scratch = [item if not isinstance(item, tuple) else pltpu.VMEM(item, F32) for item in scratch]
    specs = [HB if i in far else VM for i in range(len(args))]
    return pl.pallas_call(
        kernel,
        out_shape=outs,
        in_specs=specs,
        out_specs=[VM] * len(outs),
        scratch_shapes=scratch,
        input_output_aliases=dict(aliases),
        compiler_params=params(mebibytes),
        cost_estimate=cost and pl.CostEstimate(flops=cost, bytes_accessed=cost, transcendentals=0),
    )(*args)


def swap(values, axis, odd_pairs):
    devices = lax.axis_size(axis)
    if odd_pairs:
        pairs = [(i, (i + 1) % devices if i % 2 else (i - 1) % devices) for i in range(devices)]
    else:
        pairs = [(i, i ^ 1) for i in range(devices)]
    return lax.ppermute(values, axis, pairs)


def swap_four(t_first, t_second, x_first, x_second):
    xb = swap(x_second, "xyz", True)
    xa = swap(x_first, "xyz", False)
    tb = swap(t_second, "ta", True)
    ta = swap(t_first, "ta", False)
    return ta, tb, xa, xb


def slabs(count, rows):
    return shape((count, rows, LANES), BF16)


def swap_six(ta1, ta2, tb1, tb2, x_first, x_second):
    xb = swap(x_second, "xyz", True)
    xa = swap(x_first, "xyz", False)
    second = [swap(part, "ta", True) for part in (tb1, tb2)]
    return *(swap(part, "ta", False) for part in (ta1, ta2)), *second, xa, xb


def corners_of(fields, deep, *near):
    kernel = functools.partial(corner_kernel, fields, deep)
    *t_parts, xa, xb = near
    beyond = t_parts if deep else ()
    ca, cb = call(kernel, 4, [slabs((2 + 2 * deep) * fields, ROWS)] * 2, [], xb, xa, *beyond)
    cb = swap(cb, "ta", True)
    return swap(ca, "ta", False), cb


def per_device(source, mass, links, near_null, coarse_op, plan):
    out_shape = source.shape
    source = source.reshape(8, LT, ROWS, LANES)
    mass = mass.reshape(LT, ROWS, LANES)
    links = links.reshape(4, LT, ROWS, LANES)
    near_null = near_null.reshape(NVEC, 4, LT, ROWS, LANES)
    coarse_op = coarse_op.reshape(9, NVEC, 2 * NVEC, 32)
    count = 2 * NVEC * RHS
    field, own, ext = (8, LT, ROWS, LANES), (4, LT, 2 * ROWS, LANES), (4, ET, 2 * EROWS, LANES)
    inputs = [shape(ext, F32), shape(ext, F32), shape(ext[1:], F32)]

    plan = pltpu.with_memory_space_constraint(plan, pltpu.HBM)
    source, mass, links, x_a, x_b = call(
        load_kernel,
        8,
        [shape(field, F32), shape(field[1:], F32), shape((4, *field[1:]), I32)] + [slabs(4 * FIELDS + 8, 16)] * 2,
        [pltpu.SemaphoreType.DMA((3,))],
        *(pltpu.with_memory_space_constraint(value, pltpu.HBM) for value in (source, mass, links)),
        far=(0, 1, 2),
    )
    shares = call(share_kernel, 6, [slabs(2 * FIELDS + 4, ROWS)] * 4, [], source, mass, links, cost=1 << 22)
    near = swap_six(*shares, x_a, x_b)
    corners = corners_of(FIELDS, 0, *near)
    coarse_op = pltpu.with_memory_space_constraint(coarse_op, pltpu.HBM)
    *inputs_near, operator = call(
        cross_kernel,
        10,
        inputs + [shape(ext, F32)] * 2 + [shape((7, 6, 2 * NVEC, LANES), F32)],
        [pltpu.VMEM(coarse_op.shape, BF16), pltpu.SMEM((SWEEPS,), I32), pltpu.SemaphoreType.DMA((2,))],
        *near[::-1], source, mass, links, coarse_op, plan,
        far=(9, 10),
        cost=1 << 22,
    )
    solution, rhs, rounded, src, signs, inverse, *_ = call(
        pre_kernel,
        12,
        [shape(field, F32), shape((count, LANES), F32), shape((count, LANES), BF16)] + inputs + [shape(ext, F32)] * 2,
        [(LT, 2 * ROWS, LANES), own, (8 * count, LANES), pltpu.SMEM((SWEEPS,), I32), pltpu.SemaphoreType.DMA],
        plan, mass, *corners, *inputs_near, near_null,
        aliases=((4, 3), (5, 4), (6, 5), (7, 6), (8, 7)),
        far=(0,),
    )
    estimate = rhs
    beside = (7, count, LANES)
    for turn in range(1, KC):
        near = swap_four(rounded, rounded, rounded, rounded)
        given = (operator, rhs, estimate, rounded, *near)
        if turn < KC - 1:
            outs = [shape((count, LANES), F32), shape((count, LANES), BF16)]
            estimate, rounded = call(coarse_kernel, 6, outs, [beside], *given)
    solution, x_a, x_b = call(
        prolong_kernel,
        12,
        [shape(field, F32)] + [slabs(48, 16)] * 2,
        [beside, (count, LANES), (count, 8, LANES)],
        *given, near_null, solution,
    )
    shares = call(share_field_kernel, 4, [slabs(20, ROWS)] * 4, [], solution, cost=1 << 22)
    near = swap_six(*shares, x_a, x_b)
    corners = corners_of(8, 1, *near)
    plan_scratch = [pltpu.SMEM((SWEEPS,), I32), pltpu.SemaphoreType.DMA]
    grown = call(
        field_kernel,
        8,
        [shape(ext, F32)] * 2,
        plan_scratch,
        *near[::-1], solution, src, signs, inverse, plan,
        far=(10,),
        cost=1 << 22,
    )
    solution, residual, *_ = call(
        post_kernel,
        12,
        [shape(field, F32)] * 2 + [shape(ext, F32)] * 2,
        [(LT, 2 * ROWS, LANES), own] + plan_scratch,
        plan, mass, src, signs, inverse, *grown, *corners,
        aliases=((5, 2), (6, 3)),
        far=(0,),
    )
    return solution.reshape(out_shape), residual.reshape(out_shape)


def solution(mesh):
    return jax.shard_map(
        per_device,
        mesh=mesh,
        in_specs=(
            P(None, None, "ta", "xyz", None, None),
            P("ta", "xyz", None, None),
            P(None, "ta", "xyz", None, None),
            P(None, None, "ta", "xyz", None, None),
            P(None, None, None, "ta", "xyz", None, None),
            P(),
        ),
        out_specs=(P(None, None, "ta", "xyz", None, None), P(None, None, "ta", "xyz", None, None)),
        check_vma=False,
    )
```

```python
import functools

import jax
import jax.numpy as jnp
from jax import lax
from jax.experimental import pallas as pl
from jax.experimental.pallas import tpu as pltpu
from jax.sharding import PartitionSpec as P

LT, ROWS, LANES = 4, 32, 128
NVEC, RHS, KC, SWEEPS = 24, 2, 6, 8
ET, EROWS, PAD = 14, 80, 8
T0, OWN = 5, (24, ROWS)
FIELDS = 13
F32, BF16, I32 = jnp.float32, jnp.bfloat16, jnp.int32


def params(mebibytes):
    return pltpu.CompilerParams(vmem_limit_bytes=int(mebibytes * 1024 * 1024))


def shape(dims, dtype):
    return jax.ShapeDtypeStruct(dims, dtype)


VM = pl.BlockSpec(memory_space=pltpu.VMEM)
HB = pl.BlockSpec(memory_space=pltpu.HBM)


def roll(values, shift, axis):
    return pltpu.roll(values, shift, axis)


def tile_iotas():
    row = lax.broadcasted_iota(I32, (8, LANES), 0)
    lane = lax.broadcasted_iota(I32, (8, LANES), 1)
    return row, lane


def turns(v):
    along_y = (roll(v[0], 2, 0), roll(v[1], 6, 0), roll(v[2], 6, 0), roll(v[3], 2, 0))
    f, g = roll(v[0] + v[3], LANES - 1, 1), roll(v[1] - v[2], LANES - 1, 1)
    h, k = roll(v[0] - v[3], 1, 1), roll(v[1] + v[2], 1, 1)
    return along_y, (f, g, h, k)


def hops(turned, before, after, ahead_t, behind_t, coefs):
    sign_t, sign_x, sign_y, sign_z = coefs
    p0, p1 = ahead_t[0] - ahead_t[2], ahead_t[1] - ahead_t[3]
    q0, q1 = behind_t[0] + behind_t[2], behind_t[1] + behind_t[3]
    along_t = (q0 + p0, q1 + p1, q0 - p0, q1 - p1)
    u0, u2 = after[0] - after[1], after[2] + after[3]
    w0, w2 = before[0] + before[1], before[2] - before[3]
    along_x = (w0 + u0, w0 - u0, u2 + w2, u2 - w2)
    along_y, (f, g, h, k) = turned
    along_z = (f + h, k + g, k - g, f - h)
    return [
        (sign_t * along_t[s] + sign_x * along_x[s]) + (sign_y * along_y[s] + sign_z * along_z[s])
        for s in range(4)
    ]


def layer_rows(layer):
    start = 2 * PAD + 8 * layer
    return slice(start, start + 8)


def visit(field, signs, slices, tiles, put):
    lows = slices[0::2]
    length = slices[1] - slices[0]

    def spins_at(time, layer):
        return [field[s, time, layer_rows(layer), :] for s in range(4)]

    def layers_of(t, first, last):
        spins, turned = {first - 1: spins_at(t, first - 1)}, {}

        def prepare(layer):
            if layer <= last:
                spins[layer] = spins_at(t, layer)
            if layer < last:
                turned[layer] = turns(spins[layer])

        for layer in range(first, first + 2):
            prepare(layer)
        for layer in range(first, last):
            prepare(layer + 2)
            coefs = [signs[m, t, layer_rows(layer), :] for m in range(4)]
            sums = hops(
                turned[layer], spins[layer - 1], spins[layer + 1], spins_at(t + 1, layer), spins_at(t - 1, layer), coefs
            )
            put(t, layer, spins[layer], sums)

    def body(step, carry):
        t = step + lows[0] if len(lows) == 1 else jnp.where(step < length, step + lows[0], step - length + lows[1])
        for low, high in zip(tiles[0::2], tiles[1::2]):
            layers_of(t, 2 * low, 2 * high)
        return carry

    lax.fori_loop(0, length * len(lows), body, 0, unroll=min(4, length * len(lows)))


def chosen(plan, colour, t, layer, lane):
    block = lax.axis_index("ta") + (t + 3) // 4 + layer // 4 + 1
    return ((lane >> 2) & 1) == ((plan[colour] + block) & 1)


def half_sweep(plan, colour, target, field, source, signs, inverse, slices, tiles, lane):
    def put(t, layer, centre, sums):
        rows = layer_rows(layer)
        mask = chosen(plan, colour, t, layer, lane)
        scale = inverse[t, rows, :]
        for s in range(4):
            value = (source[s, t, rows, :] + sums[s]) * scale
            target[s, t, rows, :] = jnp.where(mask, value, centre[s])

    visit(field, signs, slices, tiles, put)


EARLY = (((6, 8), (0, 8)), ((5, 6, 8, 9), (2, 6)), ((2, 5, 9, 12), (3, 5)))
LATE = {
    3: (((5, 6, 8, 9), (0, 2, 6, 8)), ((3, 5, 9, 11), (1, 3, 5, 7)), ((2, 3, 11, 12), (2, 3, 5, 6))),
    4: (
        ((5, 6, 8, 9), (0, 2, 6, 8)),
        ((4, 5, 9, 10), (0, 3, 5, 8)),
        ((2, 4, 10, 12), (1, 3, 5, 7)),
        ((1, 2, 12, 13), (2, 6)),
    ),
}


def part_sweep(plan, colour, parts, target, field, src, signs, inverse, lane):
    for slices, tiles in parts:
        half_sweep(plan, colour, target, field, src, signs, inverse, slices, tiles, lane)


def first_values(plan, target, src, inverse, lane, low, high, layers):
    def one_slice(t, carry):
        for layer in layers:
            rows = layer_rows(layer)
            scale = jnp.where(chosen(plan, 0, t, layer, lane), inverse[t, rows, :], 0.0)
            for s in range(4):
                target[s, t, rows, :] = src[s, t, rows, :] * scale
        return carry

    lax.fori_loop(low, high, one_slice, 0)


OWN_LAYERS, HALO_LAYERS = tuple(range(4, 12)), (0, 1, 2, 3, 12, 13, 14, 15)


def wide_sweep(plan, colour, depth, target, field, src, signs, inverse, lane):
    done = 0
    while done <= depth:
        tiles = (2, 6) if depth == done else (1, 7) if depth - done <= 2 else (0, 8)
        last = depth if depth == done else depth - 1 if depth - done <= 2 else depth - 3
        if done == 0:
            slices = (T0 - last, T0 + LT + last)
        else:
            slices = (T0 - last, T0 - done + 1, T0 + LT + done - 1, T0 + LT + last)
        half_sweep(plan, colour, target, field, src, signs, inverse, slices, tiles, lane)
        done = last + 1


def places():
    t_odd, x_odd = lax.axis_index("ta") & 1, lax.axis_index("xyz") & 1
    return (t_odd, 1 - t_odd), (x_odd, 1 - x_odd)


def x_start(before):
    return PAD + 48 * (1 - before)


def side_rows(rows, n):
    return pl.ds(2 * rows[0] + n, rows[1], stride=2)


def column_of(data, t, before, first):
    pair = data[8 * (t // 2) : 8 * (t // 2) + 8]
    turned = roll(pair, 4, 0)
    top, bottom = (pair, turned) if t % 2 == 0 else (turned, pair)
    return jnp.where(before == 0, jnp.where(first, top, 0.0), jnp.where(first, 0.0, bottom))


def put_cross(fields, ta, tb, xa, xb, put, add_low, first):
    t_before, x_before = places()
    for data, before in ((ta, t_before[0]), (tb, t_before[1])):
        for part in range(2):
            base = T0 + LT - 8 * before + 2 * part

            def t_slice(t, carry, data=data[part], base=base):
                for c in range(fields):
                    put(c, base + t, OWN, data[fields * t + c].astype(F32))
                return carry

            lax.fori_loop(0, 2, t_slice, 0)
        near = T0 + LT - 5 * before
        for c in range(8):
            add_low(c, near, OWN, data[c // 4][2 * fields + c % 4].astype(F32))
    for data, before in ((xa, x_before[0]), (xb, x_before[1])):
        start = x_start(before)

        def x_slice(t, carry, data=data, start=start):
            for c in range(fields):
                put(c, T0 + t, (start, 16), data[fields * t + c].astype(F32))
            return carry

        lax.fori_loop(0, LT, x_slice, 0)
        where = (start + 8 * before, 8)
        for c in range(8):
            low = data[4 * fields + c].astype(F32)
            for t in range(LT):
                add_low(c, T0 + t, where, column_of(low, t, before, first))


def put_corners(fields, ca, cb, put, deep):
    t_before, x_before = places()
    for data, before in ((ca, t_before[0]), (cb, t_before[1])):
        near, step = T0 + LT - 5 * before, 1 - 2 * before
        for half in range(2):
            start = x_start(x_before[half])
            facing = (start + 8 * x_before[half], 8)
            part = slice(16 * half, 16 * half + 16)
            for c in range(fields):
                put(c, near, (start, 16), data[c, part, :].astype(F32))
                if deep:
                    put(c, near + step, (start, 16), data[fields + c, part, :].astype(F32))
                value = data[(1 + deep) * fields + c, part, :].astype(F32)
                put(c, near + (1 + deep) * step, facing, value[:8])
                put(c, near + (2 + deep) * step, facing, value[8:])
        if deep:
            for c in range(fields):
                put(c, (ET - 1) * (1 - before), OWN, data[3 * fields + c].astype(F32))


def low_part(value):
    return value - value.astype(BF16).astype(F32)


def pack_t(fields, read, t_a, t_b):
    t_before, _ = places()
    for part in range(2):

        def one_slice(t, carry, part=part):
            for c in range(fields):
                value = read(c, 2 * part + t).astype(BF16)
                t_a[part][fields * t + c] = value
                t_b[part][fields * t + c] = value
            return carry

        lax.fori_loop(0, 2, one_slice, 0)
    for c in range(8):
        for out, before in ((t_a, t_before[0]), (t_b, t_before[1])):
            out[c // 4][2 * fields + c % 4] = low_part(read(c, 3 * (1 - before))).astype(BF16)


def pack_x(fields, read, x_a, x_b, first):
    _, x_before = places()

    def one_slice(t, carry):
        for c in range(fields):
            value = read(c, t).astype(BF16)
            x_a[fields * t + c] = jnp.where(x_before[0] == 0, value[16:], value[:16])
            x_b[fields * t + c] = jnp.where(x_before[1] == 0, value[16:], value[:16])
        return carry

    lax.fori_loop(0, LT, one_slice, 0)

    def join(tops, bottoms):
        return jnp.concatenate([jnp.where(first, tops[t], bottoms[t + 1]) for t in (0, 2)], 0)

    def turn(values):
        return [roll(value, 4, 0) for value in values]

    for c in range(8):
        values = [read(c, t) for t in range(LT)]
        lows = [low_part(value[:8]) for value in values]
        highs = [low_part(value[24:]) for value in values]
        low, high = join(lows, turn(lows)), join(turn(highs), highs)
        for out, before in ((x_a, x_before[0]), (x_b, x_before[1])):
            out[4 * fields + c] = jnp.where(before == 0, high, low).astype(BF16)
        if x_a.shape[0] > 4 * fields + 8:
            lows = [value[16:24] for value in values]
            highs = [value[8:16] for value in values]
            low, high = join(lows, turn(lows)), join(turn(highs), highs)
            for out, before in ((x_a, x_before[0]), (x_b, x_before[1])):
                out[4 * fields + 8 + c] = jnp.where(before == 0, high, low).astype(BF16)


def corner_kernel(fields, deep, *refs):
    xb, xa, *beyond, ca, cb = refs
    t_before, x_before = places()
    for out, before, behind in ((ca, t_before[0], beyond[2:]), (cb, t_before[1], beyond[:2])):
        if deep:
            for c in range(fields):
                out[3 * fields + c] = jnp.where(before == 1, behind[0][c], behind[1][fields + c])
        near, step = 3 * (1 - before), 2 * before - 1

        def one_field(c, carry, out=out, near=near, step=step):
            for half, data in enumerate((xa, xb)):
                where = slice(16 * half, 16 * half + 16)
                for depth in range(1 + deep):
                    out[depth * fields + c, where, :] = data[fields * (near + depth * step) + c]
                pieces = []
                for depth in (1 + deep, 2 + deep):
                    value = data[fields * (near + depth * step) + c].astype(F32)
                    pieces.append(jnp.where(x_before[half] == 0, value[:8], value[8:]))
                out[(1 + deep) * fields + c, where, :] = jnp.concatenate(pieces, 0).astype(BF16)
            return carry

        lax.fori_loop(0, fields, one_field, 0)


def input_reader(source, mass, links):
    def read(c, t):
        if c < 8:
            return source[c, t]
        if c == 8:
            return mass[t]
        return (1.0 if c == 11 else 0.5) * (1 - 2 * links[c - 9, t]).astype(F32)

    return read


def field_writer(field):
    def put(c, t, rows, value):
        field[c // 2, t, side_rows(rows, c % 2), :] = value

    return put


def input_writer(src, signs, inverse):
    put_source = field_writer(src)

    def put(c, t, rows, value):
        if c < 8:
            put_source(c, t, rows, value)
            return
        if c == 8:
            value = 1.0 / (4.0 + value)
        for n in range(RHS):
            if c == 8:
                inverse[t, side_rows(rows, n), :] = value
            else:
                signs[c - 9, t, side_rows(rows, n), :] = value

    return put


def adder(field):
    def add_low(c, t, rows, value):
        where = side_rows(rows, c % 2)
        field[c // 2, t, where, :] = field[c // 2, t, where, :] + value

    return add_low


def load_kernel(source, mass, links, source_out, mass_out, links_out, x_a, x_b, sems):
    pairs = ((source, source_out), (mass, mass_out), (links, links_out))
    copies = [pltpu.make_async_copy(a, b, sems.at[i]) for i, (a, b) in enumerate(pairs)]
    for copy in copies:
        copy.start()
    for copy in copies:
        copy.wait()
    first = lax.broadcasted_iota(I32, (8, LANES), 0) < 4
    pack_x(FIELDS, input_reader(source_out, mass_out, links_out), x_a, x_b, first)


def share_kernel(source, mass, links, *shares):
    pack_t(FIELDS, input_reader(source, mass, links), shares[:2], shares[2:])


def cross_kernel(
    xb, xa, tb2, tb1, ta2, ta1, source, mass, links, coarse_far, plan_far,
    src, signs, inverse, field_a, field_b, operator,
    coarse, plan, sems,
):
    plan_copy = pltpu.make_async_copy(plan_far, plan, sems.at[0])
    plan_copy.start()
    copy = pltpu.make_async_copy(coarse_far, coarse, sems.at[1])
    copy.start()
    read, put = input_reader(source, mass, links), input_writer(src, signs, inverse)

    def own_slice(t, carry):
        for c in range(FIELDS):
            put(c, t + T0, OWN, read(c, t))
        return carry

    lax.fori_loop(0, LT, own_slice, 0)
    first = lax.broadcasted_iota(I32, (8, LANES), 0) < 4
    put_cross(FIELDS, (ta1, ta2), (tb1, tb2), xa, xb, put, adder(src), first)
    plan_copy.wait()
    _, lane = tile_iotas()
    first_values(plan, field_a, src, inverse, lane, 1, ET - 1, OWN_LAYERS)
    first_values(plan, field_a, src, inverse, lane, T0, T0 + LT, HALO_LAYERS)
    part_sweep(plan, 1, EARLY, field_b, field_a, src, signs, inverse, lane)
    copy.wait()
    relayout(coarse, operator)


def relayout(operator, result):
    def group(kk, carry):
        def block(b, q):
            return operator[b, 4 * kk + q].astype(F32)

        for place, kinds in enumerate(((0, 5, 6), (1,), (2,), (3,), (4,), (7,), (8,))):
            pieces = []
            for q in range(4):
                piece = block(kinds[0], q)
                for b in kinds[1:]:
                    piece = piece + block(b, q)
                pieces.append(piece)
            result[place, kk] = jnp.concatenate(pieces, axis=-1)
        return carry

    lax.fori_loop(0, 6, group, 0)


def exact_sum(matrix, values, left):
    high = values.astype(BF16)
    low = (values - high.astype(F32)).astype(BF16)

    def one(part):
        pair = (matrix, part) if left else (part, matrix)
        return jnp.dot(*pair, preferred_element_type=F32)

    return one(high) + one(low)


def fill_diag(mass, diag):
    for t in range(LT):
        for n in range(RHS):
            diag[t, side_rows((0, ROWS), n), :] = 4.0 + mass[t]


def copy_own(field, first_slice, rows, out):
    def one_slice(t, carry):
        for c in range(8):
            out[c, t] = field[c // 2, t + first_slice, side_rows(rows, c % 2), :]
        return carry

    lax.fori_loop(0, LT, one_slice, 0)


def pre_kernel(
    plan_far, mass, ca, cb, src_in, signs_in, inverse_in, field_a_in, field_b_in, near_null,
    out_solution, out_rhs, out_rounded, src, signs, inverse, field_a, field_b,
    diag, resid, sums, plan, sem,
):
    del src_in, signs_in, inverse_in, field_a_in, field_b_in
    plan_copy = pltpu.make_async_copy(plan_far, plan, sem)
    plan_copy.start()
    _, lane = tile_iotas()
    put_corners(FIELDS, ca, cb, input_writer(src, signs, inverse), 0)
    plan_copy.wait()

    first_values(plan, field_a, src, inverse, lane, 1, T0, HALO_LAYERS)
    first_values(plan, field_a, src, inverse, lane, T0 + LT, ET - 1, HALO_LAYERS)
    common = (src, signs, inverse, lane)
    part_sweep(plan, 1, LATE[3], field_b, field_a, *common)
    wide_sweep(plan, 2, 2, field_a, field_b, *common)
    wide_sweep(plan, 3, 1, field_b, field_a, *common)

    fill_diag(mass, diag)

    def put(t, layer, centre, hop):
        rows, inner = layer_rows(layer), slice(8 * layer - 32, 8 * layer - 24)
        for s in range(4):
            value = (src[s, t, rows, :] - diag[t - T0, inner, :] * centre[s]) + hop[s]
            resid[s, t - T0, inner, :] = value.astype(BF16).astype(F32)

    visit(field_b, signs, (T0, T0 + LT), (2, 6), put)
    copy_own(field_b, T0, OWN, out_solution)
    group = 4

    def vectors(step, carry):
        totals = {}
        for s in range(4):
            for t in range(LT):
                for block in range(2):
                    low, mid, high = 16 * block, 16 * block + 8, 16 * block + 16
                    halves = [
                        (resid[s, t, side_rows((low, 8), n), :], resid[s, t, side_rows((mid, 8), n), :]) for n in range(RHS)
                    ]
                    for i in range(group):
                        vector = near_null[group * step + i, s, t, low:high, :].astype(F32)
                        for n in range(RHS):
                            term = vector[:8] * halves[n][0] + vector[8:] * halves[n][1]
                            key = (i, n, block)
                            totals[key] = term if key not in totals else totals[key] + term
        for (i, n, block), value in totals.items():
            place = 8 * (48 * n + 2 * (group * step + i) + block)
            sums[pl.ds(pl.multiple_of(place, 8), 8), :] = value
        return carry

    lax.fori_loop(0, NVEC // group, vectors, 0)
    count = 2 * NVEC * RHS
    fold = jnp.where(
        lax.broadcasted_iota(I32, (count, 8 * count), 1) >> 3 == lax.broadcasted_iota(I32, (count, 8 * count), 0), 1.0, 0.0
    ).astype(BF16)
    spread = jnp.where(
        lax.broadcasted_iota(I32, (LANES, LANES), 0) >> 2 == lax.broadcasted_iota(I32, (LANES, LANES), 1) & 31, 1.0, 0.0
    ).astype(BF16)
    rhs = exact_sum(spread, exact_sum(fold, sums[...], True), False)
    out_rhs[...] = rhs
    out_rounded[...] = rhs.astype(BF16)


def coarse_step(operator, rhs, estimate, rounded, ta, tb, xa, xb, beside, out):
    row, lane = tile_iotas()
    t_odd, x_odd = lax.axis_index("ta") & 1, lax.axis_index("xyz") & 1
    even_row = (row & 1) == 0
    for i in range(12):
        where = slice(8 * i, 8 * i + 8)
        own = rounded[where].astype(F32)
        t_first, t_second = ta[where].astype(F32), tb[where].astype(F32)
        x_first, x_second = xa[where].astype(F32), xb[where].astype(F32)
        beside[0, where] = own
        beside[1, where] = jnp.where(t_odd == 0, t_first, t_second)
        beside[2, where] = jnp.where(t_odd == 0, t_second, t_first)
        after = jnp.where(x_odd == 0, x_first, x_second)
        before = jnp.where(x_odd == 0, x_second, x_first)
        own_up, own_down = roll(own, 7, 0), roll(own, 1, 0)
        beside[3, where] = jnp.where(even_row, own_up, roll(after, 1, 0))
        beside[4, where] = jnp.where(even_row, roll(before, 7, 0), own_down)
        beside[5, where] = roll(own, LANES - 1, 1)
        beside[6, where] = roll(own, 1, 1)
    totals = [[None] * RHS for _ in range(6)]
    for b in range(7):
        near = [[beside[b, 48 * n + 8 * j : 48 * n + 8 * j + 8, :] for j in range(6)] for n in range(RHS)]
        for kk in range(6):
            for j in range(6):
                block = operator[b, kk, 8 * j : 8 * j + 8, :]
                for n in range(RHS):
                    term = block * near[n][j]
                    totals[kk][n] = term if totals[kk][n] is None else totals[kk][n] + term
    diagonal = (lane >> 5) == (row >> 1)
    for n in range(RHS):
        for kk in range(6):
            where = slice(48 * n + 8 * kk, 48 * n + 8 * kk + 8)
            value = totals[kk][n]
            value = value + roll(value, 4, 0)
            value = value + roll(value, 2, 0)
            value = jnp.where(diagonal, value, 0.0)
            value = value + roll(value, 64, 1)
            value = value + roll(value, 32, 1)
            out[where] = estimate[where] + (rhs[where] - value)


def coarse_kernel(operator, rhs, estimate, rounded, ta, tb, xa, xb, out, out_rounded, beside):
    coarse_step(operator, rhs, estimate, rounded, ta, tb, xa, xb, beside, out)
    out_rounded[...] = out[...].astype(BF16)


def prolong_kernel(
    operator, rhs, estimate, rounded, ta, tb, xa, xb, near_null, solution,
    out, x_a, x_b,
    beside, final, spread_rows,
):
    coarse_step(operator, rhs, estimate, rounded, ta, tb, xa, xb, beside, final)
    widen = jnp.where(
        lax.broadcasted_iota(I32, (LANES, LANES), 0) == lax.broadcasted_iota(I32, (LANES, LANES), 1) >> 2, 1.0, 0.0
    ).astype(BF16)
    wide = jnp.dot(final[...].astype(BF16), widen, preferred_element_type=F32)
    for i in range(2 * NVEC * RHS):
        spread_rows[i] = jnp.broadcast_to(wide[i : i + 1, :], (8, LANES))

    def body(step, carry):
        pair, t = step // LT, step % LT
        spins = (2 * pair, 2 * pair + 1)
        for block in range(2):
            low, mid, high = 16 * block, 16 * block + 8, 16 * block + 16
            totals = {}
            for k in range(NVEC):
                weights = [spread_rows[48 * n + 2 * k + block] for n in range(RHS)]
                for i, s in enumerate(spins):
                    vector = near_null[k, s, t, low:high, :].astype(F32)
                    for n in range(RHS):
                        for part in range(2):
                            term = vector[8 * part : 8 * part + 8] * weights[n]
                            key = (i, n, part)
                            totals[key] = term if k == 0 else totals[key] + term
            for i, s in enumerate(spins):
                for n in range(RHS):
                    for part, span in enumerate((slice(low, mid), slice(mid, high))):
                        out[2 * s + n, t, span, :] = solution[2 * s + n, t, span, :] + totals[i, n, part]
        return carry

    lax.fori_loop(0, 2 * LT, body, 0)
    first = lax.broadcasted_iota(I32, (8, LANES), 0) < 4
    pack_x(8, lambda c, t: out[c, t], x_a, x_b, first)


def share_field_kernel(solution, *shares):
    pack_t(8, lambda c, t: solution[c, t], shares[:2], shares[2:])


def field_kernel(
    xb, xa, tb2, tb1, ta2, ta1, solution, src, signs, inverse, plan_far, field, swept, plan, sem
):
    plan_copy = pltpu.make_async_copy(plan_far, plan, sem)
    plan_copy.start()
    put = field_writer(field)

    def own_slice(t, carry):
        for c in range(8):
            put(c, t + T0, OWN, solution[c, t])
        return carry

    lax.fori_loop(0, LT, own_slice, 0)
    first = lax.broadcasted_iota(I32, (8, LANES), 0) < 4
    put_cross(8, (ta1, ta2), (tb1, tb2), xa, xb, put, adder(field), first)
    _, x_before = places()
    for data, before in ((xa, x_before[0]), (xb, x_before[1])):
        where = ((EROWS - 8) * (1 - before), 8)
        for c in range(8):
            layer = data[40 + c].astype(F32)
            for t in range(LT):
                put(c, T0 + t, where, column_of(layer, t, before, first))
    plan_copy.wait()
    _, lane = tile_iotas()
    part_sweep(plan, 4, EARLY, swept, field, src, signs, inverse, lane)


def post_kernel(
    plan_far, mass, src, signs, inverse, field_a_in, field_b_in, ca, cb,
    out, residual, field_a, field_b,
    diag, resid, plan, sem,
):
    del field_a_in, field_b_in
    plan_copy = pltpu.make_async_copy(plan_far, plan, sem)
    plan_copy.start()
    row, lane = tile_iotas()

    put_corners(8, ca, cb, field_writer(field_a), 1)
    fill_diag(mass, diag)
    plan_copy.wait()
    common = (src, signs, inverse, lane)
    part_sweep(plan, 4, LATE[4], field_b, field_a, *common)
    wide_sweep(plan, 5, 3, field_a, field_b, *common)
    wide_sweep(plan, 6, 2, field_b, field_a, *common)
    wide_sweep(plan, 7, 1, field_a, field_b, *common)

    def put(t, layer, centre, hop):
        rows, inner = layer_rows(layer), slice(8 * layer - 32, 8 * layer - 24)
        for s in range(4):
            resid[s, t - T0, inner, :] = (src[s, t, rows, :] - diag[t - T0, inner, :] * centre[s]) + hop[s]

    visit(field_a, signs, (T0, T0 + LT), (2, 6), put)
    copy_own(field_a, T0, OWN, out)
    copy_own(resid, 0, (0, ROWS), residual)


def call(kernel, mebibytes, outs, scratch, *args, aliases=(), far=(), cost=None):
    scratch = [item if not isinstance(item, tuple) else pltpu.VMEM(item, F32) for item in scratch]
    specs = [HB if i in far else VM for i in range(len(args))]
    return pl.pallas_call(
        kernel,
        out_shape=outs,
        in_specs=specs,
        out_specs=[VM] * len(outs),
        scratch_shapes=scratch,
        input_output_aliases=dict(aliases),
        compiler_params=params(mebibytes),
        cost_estimate=cost and pl.CostEstimate(flops=cost, bytes_accessed=cost, transcendentals=0),
    )(*args)


def swap(values, axis, odd_pairs):
    devices = lax.axis_size(axis)
    if odd_pairs:
        pairs = [(i, (i + 1) % devices if i % 2 else (i - 1) % devices) for i in range(devices)]
    else:
        pairs = [(i, i ^ 1) for i in range(devices)]
    return lax.ppermute(values, axis, pairs)


def swap_four(t_first, t_second, x_first, x_second):
    xb = swap(x_second, "xyz", True)
    xa = swap(x_first, "xyz", False)
    tb = swap(t_second, "ta", True)
    ta = swap(t_first, "ta", False)
    return ta, tb, xa, xb


def slabs(count, rows):
    return shape((count, rows, LANES), BF16)


def swap_six(ta1, ta2, tb1, tb2, x_first, x_second):
    xb = swap(x_second, "xyz", True)
    xa = swap(x_first, "xyz", False)
    second = [swap(part, "ta", True) for part in (tb1, tb2)]
    return *(swap(part, "ta", False) for part in (ta1, ta2)), *second, xa, xb


def corners_of(fields, deep, *near):
    kernel = functools.partial(corner_kernel, fields, deep)
    *t_parts, xa, xb = near
    beyond = t_parts if deep else ()
    ca, cb = call(kernel, 4, [slabs((2 + 2 * deep) * fields, ROWS)] * 2, [], xb, xa, *beyond)
    cb = swap(cb, "ta", True)
    return swap(ca, "ta", False), cb


def per_device(source, mass, links, near_null, coarse_op, plan):
    out_shape = source.shape
    source = source.reshape(8, LT, ROWS, LANES)
    mass = mass.reshape(LT, ROWS, LANES)
    links = links.reshape(4, LT, ROWS, LANES)
    near_null = near_null.reshape(NVEC, 4, LT, ROWS, LANES)
    coarse_op = coarse_op.reshape(9, NVEC, 2 * NVEC, 32)
    count = 2 * NVEC * RHS
    field, own, ext = (8, LT, ROWS, LANES), (4, LT, 2 * ROWS, LANES), (4, ET, 2 * EROWS, LANES)
    inputs = [shape(ext, F32), shape(ext, F32), shape(ext[1:], F32)]

    plan = pltpu.with_memory_space_constraint(plan, pltpu.HBM)
    source, mass, links, x_a, x_b = call(
        load_kernel,
        8,
        [shape(field, F32), shape(field[1:], F32), shape((4, *field[1:]), I32)] + [slabs(4 * FIELDS + 8, 16)] * 2,
        [pltpu.SemaphoreType.DMA((3,))],
        *(pltpu.with_memory_space_constraint(value, pltpu.HBM) for value in (source, mass, links)),
        far=(0, 1, 2),
    )
    shares = call(share_kernel, 6, [slabs(2 * FIELDS + 4, ROWS)] * 4, [], source, mass, links, cost=1 << 22)
    near = swap_six(*shares, x_a, x_b)
    corners = corners_of(FIELDS, 0, *near)
    coarse_op = pltpu.with_memory_space_constraint(coarse_op, pltpu.HBM)
    *inputs_near, operator = call(
        cross_kernel,
        10,
        inputs + [shape(ext, F32)] * 2 + [shape((7, 6, 2 * NVEC, LANES), F32)],
        [pltpu.VMEM(coarse_op.shape, BF16), pltpu.SMEM((SWEEPS,), I32), pltpu.SemaphoreType.DMA((2,))],
        *near[::-1], source, mass, links, coarse_op, plan,
        far=(9, 10),
        cost=1 << 22,
    )
    solution, rhs, rounded, src, signs, inverse, *_ = call(
        pre_kernel,
        12,
        [shape(field, F32), shape((count, LANES), F32), shape((count, LANES), BF16)] + inputs + [shape(ext, F32)] * 2,
        [(LT, 2 * ROWS, LANES), own, (8 * count, LANES), pltpu.SMEM((SWEEPS,), I32), pltpu.SemaphoreType.DMA],
        plan, mass, *corners, *inputs_near, near_null,
        aliases=((4, 3), (5, 4), (6, 5), (7, 6), (8, 7)),
        far=(0,),
    )
    estimate = rhs
    beside = (7, count, LANES)
    for turn in range(1, KC):
        near = swap_four(rounded, rounded, rounded, rounded)
        given = (operator, rhs, estimate, rounded, *near)
        if turn < KC - 1:
            outs = [shape((count, LANES), F32), shape((count, LANES), BF16)]
            estimate, rounded = call(coarse_kernel, 6, outs, [beside], *given)
    solution, x_a, x_b = call(
        prolong_kernel,
        12,
        [shape(field, F32)] + [slabs(48, 16)] * 2,
        [beside, (count, LANES), (count, 8, LANES)],
        *given, near_null, solution,
    )
    shares = call(share_field_kernel, 4, [slabs(20, ROWS)] * 4, [], solution, cost=1 << 22)
    near = swap_six(*shares, x_a, x_b)
    corners = corners_of(8, 1, *near)
    plan_scratch = [pltpu.SMEM((SWEEPS,), I32), pltpu.SemaphoreType.DMA]
    grown = call(
        field_kernel,
        8,
        [shape(ext, F32)] * 2,
        plan_scratch,
        *near[::-1], solution, src, signs, inverse, plan,
        far=(10,),
        cost=1 << 22,
    )
    solution, residual, *_ = call(
        post_kernel,
        12,
        [shape(field, F32)] * 2 + [shape(ext, F32)] * 2,
        [(LT, 2 * ROWS, LANES), own] + plan_scratch,
        plan, mass, src, signs, inverse, *grown, *corners,
        aliases=((5, 2), (6, 3)),
        far=(0,),
    )
    return solution.reshape(out_shape), residual.reshape(out_shape)


def solution(mesh):
    return jax.shard_map(
        per_device,
        mesh=mesh,
        in_specs=(
            P(None, None, "ta", "xyz", None, None),
            P("ta", "xyz", None, None),
            P(None, "ta", "xyz", None, None),
            P(None, None, "ta", "xyz", None, None),
            P(None, None, None, "ta", "xyz", None, None),
            P(),
        ),
        out_specs=(P(None, None, "ta", "xyz", None, None), P(None, None, "ta", "xyz", None, None)),
        check_vma=False,
    )
```

```python
import functools

import jax
import jax.numpy as jnp
from jax import lax
from jax.experimental import pallas as pl
from jax.experimental.pallas import tpu as pltpu
from jax.sharding import PartitionSpec as P

LT, ROWS, LANES = 4, 32, 128
NVEC, RHS, KC, SWEEPS = 24, 2, 6, 8
ET, EROWS, PAD = 14, 80, 8
T0, OWN = 5, (24, ROWS)
FIELDS = 13
F32, BF16, I32 = jnp.float32, jnp.bfloat16, jnp.int32


def params(mebibytes):
    return pltpu.CompilerParams(vmem_limit_bytes=int(mebibytes * 1024 * 1024))


def shape(dims, dtype):
    return jax.ShapeDtypeStruct(dims, dtype)


VM = pl.BlockSpec(memory_space=pltpu.VMEM)
HB = pl.BlockSpec(memory_space=pltpu.HBM)


def roll(values, shift, axis):
    return pltpu.roll(values, shift, axis)


def tile_iotas():
    row = lax.broadcasted_iota(I32, (8, LANES), 0)
    lane = lax.broadcasted_iota(I32, (8, LANES), 1)
    return row, lane


def turns(v):
    along_y = (roll(v[0], 2, 0), roll(v[1], 6, 0), roll(v[2], 6, 0), roll(v[3], 2, 0))
    f, g = roll(v[0] + v[3], LANES - 1, 1), roll(v[1] - v[2], LANES - 1, 1)
    h, k = roll(v[0] - v[3], 1, 1), roll(v[1] + v[2], 1, 1)
    return along_y, (f, g, h, k)


def hops(turned, before, after, ahead_t, behind_t, coefs):
    sign_t, sign_x, sign_y, sign_z = coefs
    p0, p1 = ahead_t[0] - ahead_t[2], ahead_t[1] - ahead_t[3]
    q0, q1 = behind_t[0] + behind_t[2], behind_t[1] + behind_t[3]
    along_t = (q0 + p0, q1 + p1, q0 - p0, q1 - p1)
    u0, u2 = after[0] - after[1], after[2] + after[3]
    w0, w2 = before[0] + before[1], before[2] - before[3]
    along_x = (w0 + u0, w0 - u0, u2 + w2, u2 - w2)
    along_y, (f, g, h, k) = turned
    along_z = (f + h, k + g, k - g, f - h)
    return [
        (sign_t * along_t[s] + sign_x * along_x[s]) + (sign_y * along_y[s] + sign_z * along_z[s])
        for s in range(4)
    ]


def layer_rows(layer):
    start = 2 * PAD + 8 * layer
    return slice(start, start + 8)


def visit(field, signs, slices, tiles, put):
    lows = slices[0::2]
    length = slices[1] - slices[0]

    def spins_at(time, layer):
        return [field[s, time, layer_rows(layer), :] for s in range(4)]

    def layers_of(t, first, last):
        spins, turned = {first - 1: spins_at(t, first - 1)}, {}

        def prepare(layer):
            if layer <= last:
                spins[layer] = spins_at(t, layer)
            if layer < last:
                turned[layer] = turns(spins[layer])

        for layer in range(first, first + 2):
            prepare(layer)
        for layer in range(first, last):
            prepare(layer + 2)
            coefs = [signs[m, t, layer_rows(layer), :] for m in range(4)]
            sums = hops(
                turned[layer], spins[layer - 1], spins[layer + 1], spins_at(t + 1, layer), spins_at(t - 1, layer), coefs
            )
            put(t, layer, spins[layer], sums)

    def body(step, carry):
        t = step + lows[0] if len(lows) == 1 else jnp.where(step < length, step + lows[0], step - length + lows[1])
        for low, high in zip(tiles[0::2], tiles[1::2]):
            layers_of(t, 2 * low, 2 * high)
        return carry

    lax.fori_loop(0, length * len(lows), body, 0, unroll=min(4, length * len(lows)))


def chosen(plan, colour, t, layer, lane):
    block = lax.axis_index("ta") + (t + 3) // 4 + layer // 4 + 1
    return ((lane >> 2) & 1) == ((plan[colour] + block) & 1)


def half_sweep(plan, colour, target, field, source, signs, inverse, slices, tiles, lane):
    def put(t, layer, centre, sums):
        rows = layer_rows(layer)
        mask = chosen(plan, colour, t, layer, lane)
        scale = inverse[t, rows, :]
        for s in range(4):
            value = (source[s, t, rows, :] + sums[s]) * scale
            target[s, t, rows, :] = jnp.where(mask, value, centre[s])

    visit(field, signs, slices, tiles, put)


EARLY = (((6, 8), (0, 8)), ((5, 6, 8, 9), (2, 6)), ((2, 5, 9, 12), (3, 5)))
LATE = {
    3: (((5, 6, 8, 9), (0, 2, 6, 8)), ((3, 5, 9, 11), (1, 3, 5, 7)), ((2, 3, 11, 12), (2, 3, 5, 6))),
    4: (
        ((5, 6, 8, 9), (0, 2, 6, 8)),
        ((4, 5, 9, 10), (0, 3, 5, 8)),
        ((2, 4, 10, 12), (1, 3, 5, 7)),
        ((1, 2, 12, 13), (2, 6)),
    ),
}


def part_sweep(plan, colour, parts, target, field, src, signs, inverse, lane):
    for slices, tiles in parts:
        half_sweep(plan, colour, target, field, src, signs, inverse, slices, tiles, lane)


def first_values(plan, target, src, inverse, lane, low, high, layers):
    def one_slice(t, carry):
        for layer in layers:
            rows = layer_rows(layer)
            scale = jnp.where(chosen(plan, 0, t, layer, lane), inverse[t, rows, :], 0.0)
            for s in range(4):
                target[s, t, rows, :] = src[s, t, rows, :] * scale
        return carry

    lax.fori_loop(low, high, one_slice, 0)


OWN_LAYERS, HALO_LAYERS = tuple(range(4, 12)), (0, 1, 2, 3, 12, 13, 14, 15)


def wide_sweep(plan, colour, depth, target, field, src, signs, inverse, lane):
    done = 0
    while done <= depth:
        tiles = (2, 6) if depth == done else (1, 7) if depth - done <= 2 else (0, 8)
        last = depth if depth == done else depth - 1 if depth - done <= 2 else depth - 3
        if done == 0:
            slices = (T0 - last, T0 + LT + last)
        else:
            slices = (T0 - last, T0 - done + 1, T0 + LT + done - 1, T0 + LT + last)
        half_sweep(plan, colour, target, field, src, signs, inverse, slices, tiles, lane)
        done = last + 1


def places():
    t_odd, x_odd = lax.axis_index("ta") & 1, lax.axis_index("xyz") & 1
    return (t_odd, 1 - t_odd), (x_odd, 1 - x_odd)


def x_start(before):
    return PAD + 48 * (1 - before)


def side_rows(rows, n):
    return pl.ds(2 * rows[0] + n, rows[1], stride=2)


def column_of(data, t, before, first):
    pair = data[8 * (t // 2) : 8 * (t // 2) + 8]
    turned = roll(pair, 4, 0)
    top, bottom = (pair, turned) if t % 2 == 0 else (turned, pair)
    return jnp.where(before == 0, jnp.where(first, top, 0.0), jnp.where(first, 0.0, bottom))


def put_cross(fields, ta, tb, xa, xb, put, add_low, first):
    t_before, x_before = places()
    for data, before in ((ta, t_before[0]), (tb, t_before[1])):
        for part in range(2):
            base = T0 + LT - 8 * before + 2 * part

            def t_slice(t, carry, data=data[part], base=base):
                for c in range(fields):
                    put(c, base + t, OWN, data[fields * t + c].astype(F32))
                return carry

            lax.fori_loop(0, 2, t_slice, 0)
        near = T0 + LT - 5 * before
        for c in range(8):
            add_low(c, near, OWN, data[c // 4][2 * fields + c % 4].astype(F32))
    for data, before in ((xa, x_before[0]), (xb, x_before[1])):
        start = x_start(before)

        def x_slice(t, carry, data=data, start=start):
            for c in range(fields):
                put(c, T0 + t, (start, 16), data[fields * t + c].astype(F32))
            return carry

        lax.fori_loop(0, LT, x_slice, 0)
        where = (start + 8 * before, 8)
        for c in range(8):
            low = data[4 * fields + c].astype(F32)
            for t in range(LT):
                add_low(c, T0 + t, where, column_of(low, t, before, first))


def put_corners(fields, ca, cb, put, deep):
    t_before, x_before = places()
    for data, before in ((ca, t_before[0]), (cb, t_before[1])):
        near, step = T0 + LT - 5 * before, 1 - 2 * before
        for half in range(2):
            start = x_start(x_before[half])
            facing = (start + 8 * x_before[half], 8)
            part = slice(16 * half, 16 * half + 16)
            for c in range(fields):
                put(c, near, (start, 16), data[c, part, :].astype(F32))
                if deep:
                    put(c, near + step, (start, 16), data[fields + c, part, :].astype(F32))
                value = data[(1 + deep) * fields + c, part, :].astype(F32)
                put(c, near + (1 + deep) * step, facing, value[:8])
                put(c, near + (2 + deep) * step, facing, value[8:])
        if deep:
            for c in range(fields):
                put(c, (ET - 1) * (1 - before), OWN, data[3 * fields + c].astype(F32))


def low_part(value):
    return value - value.astype(BF16).astype(F32)


def pack_t(fields, read, t_a, t_b):
    t_before, _ = places()
    for part in range(2):

        def one_slice(t, carry, part=part):
            for c in range(fields):
                value = read(c, 2 * part + t).astype(BF16)
                t_a[part][fields * t + c] = value
                t_b[part][fields * t + c] = value
            return carry

        lax.fori_loop(0, 2, one_slice, 0)
    for c in range(8):
        for out, before in ((t_a, t_before[0]), (t_b, t_before[1])):
            out[c // 4][2 * fields + c % 4] = low_part(read(c, 3 * (1 - before))).astype(BF16)


def pack_x(fields, read, x_a, x_b, first):
    _, x_before = places()

    def one_slice(t, carry):
        for c in range(fields):
            value = read(c, t).astype(BF16)
            x_a[fields * t + c] = jnp.where(x_before[0] == 0, value[16:], value[:16])
            x_b[fields * t + c] = jnp.where(x_before[1] == 0, value[16:], value[:16])
        return carry

    lax.fori_loop(0, LT, one_slice, 0)

    def join(tops, bottoms):
        return jnp.concatenate([jnp.where(first, tops[t], bottoms[t + 1]) for t in (0, 2)], 0)

    def turn(values):
        return [roll(value, 4, 0) for value in values]

    for c in range(8):
        values = [read(c, t) for t in range(LT)]
        lows = [low_part(value[:8]) for value in values]
        highs = [low_part(value[24:]) for value in values]
        low, high = join(lows, turn(lows)), join(turn(highs), highs)
        for out, before in ((x_a, x_before[0]), (x_b, x_before[1])):
            out[4 * fields + c] = jnp.where(before == 0, high, low).astype(BF16)
        if x_a.shape[0] > 4 * fields + 8:
            lows = [value[16:24] for value in values]
            highs = [value[8:16] for value in values]
            low, high = join(lows, turn(lows)), join(turn(highs), highs)
            for out, before in ((x_a, x_before[0]), (x_b, x_before[1])):
                out[4 * fields + 8 + c] = jnp.where(before == 0, high, low).astype(BF16)


def corner_kernel(fields, deep, *refs):
    xb, xa, *beyond, ca, cb = refs
    t_before, x_before = places()
    for out, before, behind in ((ca, t_before[0], beyond[2:]), (cb, t_before[1], beyond[:2])):
        if deep:
            for c in range(fields):
                out[3 * fields + c] = jnp.where(before == 1, behind[0][c], behind[1][fields + c])
        near, step = 3 * (1 - before), 2 * before - 1

        def one_field(c, carry, out=out, near=near, step=step):
            for half, data in enumerate((xa, xb)):
                where = slice(16 * half, 16 * half + 16)
                for depth in range(1 + deep):
                    out[depth * fields + c, where, :] = data[fields * (near + depth * step) + c]
                pieces = []
                for depth in (1 + deep, 2 + deep):
                    value = data[fields * (near + depth * step) + c].astype(F32)
                    pieces.append(jnp.where(x_before[half] == 0, value[:8], value[8:]))
                out[(1 + deep) * fields + c, where, :] = jnp.concatenate(pieces, 0).astype(BF16)
            return carry

        lax.fori_loop(0, fields, one_field, 0)


def input_reader(source, mass, links):
    def read(c, t):
        if c < 8:
            return source[c, t]
        if c == 8:
            return mass[t]
        return (1.0 if c == 11 else 0.5) * (1 - 2 * links[c - 9, t]).astype(F32)

    return read


def field_writer(field):
    def put(c, t, rows, value):
        field[c // 2, t, side_rows(rows, c % 2), :] = value

    return put


def input_writer(src, signs, inverse):
    put_source = field_writer(src)

    def put(c, t, rows, value):
        if c < 8:
            put_source(c, t, rows, value)
            return
        if c == 8:
            value = 1.0 / (4.0 + value)
        for n in range(RHS):
            if c == 8:
                inverse[t, side_rows(rows, n), :] = value
            else:
                signs[c - 9, t, side_rows(rows, n), :] = value

    return put


def adder(field):
    def add_low(c, t, rows, value):
        where = side_rows(rows, c % 2)
        field[c // 2, t, where, :] = field[c // 2, t, where, :] + value

    return add_low


def load_kernel(source, mass, links, source_out, mass_out, links_out, x_a, x_b, sems):
    pairs = ((source, source_out), (mass, mass_out), (links, links_out))
    copies = [pltpu.make_async_copy(a, b, sems.at[i]) for i, (a, b) in enumerate(pairs)]
    for copy in copies:
        copy.start()
    for copy in copies:
        copy.wait()
    first = lax.broadcasted_iota(I32, (8, LANES), 0) < 4
    pack_x(FIELDS, input_reader(source_out, mass_out, links_out), x_a, x_b, first)


def share_kernel(source, mass, links, *shares):
    pack_t(FIELDS, input_reader(source, mass, links), shares[:2], shares[2:])


def cross_kernel(
    xb, xa, tb2, tb1, ta2, ta1, source, mass, links, coarse_far, plan_far,
    src, signs, inverse, field_a, field_b, operator,
    coarse, plan, sems,
):
    plan_copy = pltpu.make_async_copy(plan_far, plan, sems.at[0])
    plan_copy.start()
    copy = pltpu.make_async_copy(coarse_far, coarse, sems.at[1])
    copy.start()
    read, put = input_reader(source, mass, links), input_writer(src, signs, inverse)

    def own_slice(t, carry):
        for c in range(FIELDS):
            put(c, t + T0, OWN, read(c, t))
        return carry

    lax.fori_loop(0, LT, own_slice, 0)
    first = lax.broadcasted_iota(I32, (8, LANES), 0) < 4
    put_cross(FIELDS, (ta1, ta2), (tb1, tb2), xa, xb, put, adder(src), first)
    plan_copy.wait()
    _, lane = tile_iotas()
    first_values(plan, field_a, src, inverse, lane, 1, ET - 1, OWN_LAYERS)
    first_values(plan, field_a, src, inverse, lane, T0, T0 + LT, HALO_LAYERS)
    part_sweep(plan, 1, EARLY, field_b, field_a, src, signs, inverse, lane)
    copy.wait()
    relayout(coarse, operator)


def relayout(operator, result):
    def group(kk, carry):
        def block(b, q):
            return operator[b, 4 * kk + q].astype(F32)

        for place, kinds in enumerate(((0, 5, 6), (1,), (2,), (3,), (4,), (7,), (8,))):
            pieces = []
            for q in range(4):
                piece = block(kinds[0], q)
                for b in kinds[1:]:
                    piece = piece + block(b, q)
                pieces.append(piece)
            result[place, kk] = jnp.concatenate(pieces, axis=-1)
        return carry

    lax.fori_loop(0, 6, group, 0)


def exact_sum(matrix, values, left):
    high = values.astype(BF16)
    low = (values - high.astype(F32)).astype(BF16)

    def one(part):
        pair = (matrix, part) if left else (part, matrix)
        return jnp.dot(*pair, preferred_element_type=F32)

    return one(high) + one(low)


def fill_diag(mass, diag):
    for t in range(LT):
        for n in range(RHS):
            diag[t, side_rows((0, ROWS), n), :] = 4.0 + mass[t]


def copy_own(field, first_slice, rows, out):
    def one_slice(t, carry):
        for c in range(8):
            out[c, t] = field[c // 2, t + first_slice, side_rows(rows, c % 2), :]
        return carry

    lax.fori_loop(0, LT, one_slice, 0)


def pre_kernel(
    plan_far, mass, ca, cb, src_in, signs_in, inverse_in, field_a_in, field_b_in, near_null,
    out_solution, out_rhs, out_rounded, out_sent, src, signs, inverse, field_a, field_b,
    diag, resid, sums, plan, sem,
):
    del src_in, signs_in, inverse_in, field_a_in, field_b_in
    plan_copy = pltpu.make_async_copy(plan_far, plan, sem)
    plan_copy.start()
    _, lane = tile_iotas()
    put_corners(FIELDS, ca, cb, input_writer(src, signs, inverse), 0)
    plan_copy.wait()

    first_values(plan, field_a, src, inverse, lane, 1, T0, HALO_LAYERS)
    first_values(plan, field_a, src, inverse, lane, T0 + LT, ET - 1, HALO_LAYERS)
    common = (src, signs, inverse, lane)
    part_sweep(plan, 1, LATE[3], field_b, field_a, *common)
    wide_sweep(plan, 2, 2, field_a, field_b, *common)
    wide_sweep(plan, 3, 1, field_b, field_a, *common)

    fill_diag(mass, diag)

    def put(t, layer, centre, hop):
        rows, inner = layer_rows(layer), slice(8 * layer - 32, 8 * layer - 24)
        for s in range(4):
            value = (src[s, t, rows, :] - diag[t - T0, inner, :] * centre[s]) + hop[s]
            resid[s, t - T0, inner, :] = value.astype(BF16).astype(F32)

    visit(field_b, signs, (T0, T0 + LT), (2, 6), put)
    copy_own(field_b, T0, OWN, out_solution)
    group = 4

    def vectors(step, carry):
        totals = {}
        for s in range(4):
            for t in range(LT):
                for block in range(2):
                    low, mid, high = 16 * block, 16 * block + 8, 16 * block + 16
                    halves = [
                        (resid[s, t, side_rows((low, 8), n), :], resid[s, t, side_rows((mid, 8), n), :]) for n in range(RHS)
                    ]
                    for i in range(group):
                        vector = near_null[group * step + i, s, t, low:high, :].astype(F32)
                        for n in range(RHS):
                            term = vector[:8] * halves[n][0] + vector[8:] * halves[n][1]
                            key = (i, n, block)
                            totals[key] = term if key not in totals else totals[key] + term
        for (i, n, block), value in totals.items():
            place = 8 * (48 * n + 2 * (group * step + i) + block)
            sums[pl.ds(pl.multiple_of(place, 8), 8), :] = value
        return carry

    lax.fori_loop(0, NVEC // group, vectors, 0)
    count = 2 * NVEC * RHS
    fold = jnp.where(
        lax.broadcasted_iota(I32, (count, 8 * count), 1) >> 3 == lax.broadcasted_iota(I32, (count, 8 * count), 0), 1.0, 0.0
    ).astype(BF16)
    spread = jnp.where(
        lax.broadcasted_iota(I32, (LANES, LANES), 0) >> 2 == lax.broadcasted_iota(I32, (LANES, LANES), 1) & 31, 1.0, 0.0
    ).astype(BF16)
    rhs = exact_sum(spread, exact_sum(fold, sums[...], True), False)
    out_rhs[...] = rhs
    out_rounded[...] = rhs.astype(BF16)
    out_sent[...] = compact(rhs, lane >> 5)


def compact(values, group):
    tiles = [values[8 * i : 8 * i + 8] for i in range(12)]
    parts = []
    for first in (0, 4, 8):
        value = tiles[first]
        for g in range(1, 4):
            value = jnp.where(group == g, tiles[first + g], value)
        parts.append(value)
    return jnp.concatenate(parts + [jnp.zeros_like(parts[0])], 0).astype(BF16)


def expand(data, group):
    values = data.astype(F32)
    tiles = []
    for i in range(12):
        value = jnp.where(group == i % 4, values[8 * (i // 4) : 8 * (i // 4) + 8], 0.0)
        value = value + roll(value, 64, 1)
        tiles.append(value + roll(value, 32, 1))
    return tiles


def coarse_step(operator, rhs, estimate, rounded, ta, tb, xa, xb, beside, out):
    row, lane = tile_iotas()
    t_odd, x_odd = lax.axis_index("ta") & 1, lax.axis_index("xyz") & 1
    even_row = (row & 1) == 0
    ta, tb, xa, xb = (expand(data[...], lane >> 5) for data in (ta, tb, xa, xb))
    for i in range(12):
        where = slice(8 * i, 8 * i + 8)
        own = rounded[where].astype(F32)
        t_first, t_second, x_first, x_second = ta[i], tb[i], xa[i], xb[i]
        beside[0, where] = own
        beside[1, where] = jnp.where(t_odd == 0, t_first, t_second)
        beside[2, where] = jnp.where(t_odd == 0, t_second, t_first)
        after = jnp.where(x_odd == 0, x_first, x_second)
        before = jnp.where(x_odd == 0, x_second, x_first)
        own_up, own_down = roll(own, 7, 0), roll(own, 1, 0)
        beside[3, where] = jnp.where(even_row, own_up, roll(after, 1, 0))
        beside[4, where] = jnp.where(even_row, roll(before, 7, 0), own_down)
        beside[5, where] = roll(own, LANES - 1, 1)
        beside[6, where] = roll(own, 1, 1)
    totals = [[None] * RHS for _ in range(6)]
    for b in range(7):
        near = [[beside[b, 48 * n + 8 * j : 48 * n + 8 * j + 8, :] for j in range(6)] for n in range(RHS)]
        for kk in range(6):
            for j in range(6):
                block = operator[b, kk, 8 * j : 8 * j + 8, :]
                for n in range(RHS):
                    term = block * near[n][j]
                    totals[kk][n] = term if totals[kk][n] is None else totals[kk][n] + term
    diagonal = (lane >> 5) == (row >> 1)
    for n in range(RHS):
        for kk in range(6):
            where = slice(48 * n + 8 * kk, 48 * n + 8 * kk + 8)
            value = totals[kk][n]
            value = value + roll(value, 4, 0)
            value = value + roll(value, 2, 0)
            value = jnp.where(diagonal, value, 0.0)
            value = value + roll(value, 64, 1)
            value = value + roll(value, 32, 1)
            out[where] = estimate[where] + (rhs[where] - value)


def coarse_kernel(operator, rhs, estimate, rounded, ta, tb, xa, xb, out, out_rounded, out_sent, beside):
    coarse_step(operator, rhs, estimate, rounded, ta, tb, xa, xb, beside, out)
    out_rounded[...] = out[...].astype(BF16)
    out_sent[...] = compact(out[...], tile_iotas()[1] >> 5)


def prolong_kernel(
    operator, rhs, estimate, rounded, ta, tb, xa, xb, near_null, solution,
    out, x_a, x_b,
    beside, final, spread_rows,
):
    coarse_step(operator, rhs, estimate, rounded, ta, tb, xa, xb, beside, final)
    widen = jnp.where(
        lax.broadcasted_iota(I32, (LANES, LANES), 0) == lax.broadcasted_iota(I32, (LANES, LANES), 1) >> 2, 1.0, 0.0
    ).astype(BF16)
    wide = jnp.dot(final[...].astype(BF16), widen, preferred_element_type=F32)
    for i in range(2 * NVEC * RHS):
        spread_rows[i] = jnp.broadcast_to(wide[i : i + 1, :], (8, LANES))

    def body(step, carry):
        pair, t = step // LT, step % LT
        spins = (2 * pair, 2 * pair + 1)
        for block in range(2):
            low, mid, high = 16 * block, 16 * block + 8, 16 * block + 16
            totals = {}
            for k in range(NVEC):
                weights = [spread_rows[48 * n + 2 * k + block] for n in range(RHS)]
                for i, s in enumerate(spins):
                    vector = near_null[k, s, t, low:high, :].astype(F32)
                    for n in range(RHS):
                        for part in range(2):
                            term = vector[8 * part : 8 * part + 8] * weights[n]
                            key = (i, n, part)
                            totals[key] = term if k == 0 else totals[key] + term
            for i, s in enumerate(spins):
                for n in range(RHS):
                    for part, span in enumerate((slice(low, mid), slice(mid, high))):
                        out[2 * s + n, t, span, :] = solution[2 * s + n, t, span, :] + totals[i, n, part]
        return carry

    lax.fori_loop(0, 2 * LT, body, 0)
    first = lax.broadcasted_iota(I32, (8, LANES), 0) < 4
    pack_x(8, lambda c, t: out[c, t], x_a, x_b, first)


def share_field_kernel(solution, *shares):
    pack_t(8, lambda c, t: solution[c, t], shares[:2], shares[2:])


def field_kernel(
    xb, xa, tb2, tb1, ta2, ta1, solution, src, signs, inverse, plan_far, field, swept, plan, sem
):
    plan_copy = pltpu.make_async_copy(plan_far, plan, sem)
    plan_copy.start()
    put = field_writer(field)

    def own_slice(t, carry):
        for c in range(8):
            put(c, t + T0, OWN, solution[c, t])
        return carry

    lax.fori_loop(0, LT, own_slice, 0)
    first = lax.broadcasted_iota(I32, (8, LANES), 0) < 4
    put_cross(8, (ta1, ta2), (tb1, tb2), xa, xb, put, adder(field), first)
    _, x_before = places()
    for data, before in ((xa, x_before[0]), (xb, x_before[1])):
        where = ((EROWS - 8) * (1 - before), 8)
        for c in range(8):
            layer = data[40 + c].astype(F32)
            for t in range(LT):
                put(c, T0 + t, where, column_of(layer, t, before, first))
    plan_copy.wait()
    _, lane = tile_iotas()
    part_sweep(plan, 4, EARLY, swept, field, src, signs, inverse, lane)


def post_kernel(
    plan_far, mass, src, signs, inverse, field_a_in, field_b_in, ca, cb,
    out, residual, field_a, field_b,
    diag, resid, plan, sem,
):
    del field_a_in, field_b_in
    plan_copy = pltpu.make_async_copy(plan_far, plan, sem)
    plan_copy.start()
    row, lane = tile_iotas()

    put_corners(8, ca, cb, field_writer(field_a), 1)
    fill_diag(mass, diag)
    plan_copy.wait()
    common = (src, signs, inverse, lane)
    part_sweep(plan, 4, LATE[4], field_b, field_a, *common)
    wide_sweep(plan, 5, 3, field_a, field_b, *common)
    wide_sweep(plan, 6, 2, field_b, field_a, *common)
    wide_sweep(plan, 7, 1, field_a, field_b, *common)

    def put(t, layer, centre, hop):
        rows, inner = layer_rows(layer), slice(8 * layer - 32, 8 * layer - 24)
        for s in range(4):
            resid[s, t - T0, inner, :] = (src[s, t, rows, :] - diag[t - T0, inner, :] * centre[s]) + hop[s]

    visit(field_a, signs, (T0, T0 + LT), (2, 6), put)
    copy_own(field_a, T0, OWN, out)
    copy_own(resid, 0, (0, ROWS), residual)


def call(kernel, mebibytes, outs, scratch, *args, aliases=(), far=(), cost=None):
    scratch = [item if not isinstance(item, tuple) else pltpu.VMEM(item, F32) for item in scratch]
    specs = [HB if i in far else VM for i in range(len(args))]
    return pl.pallas_call(
        kernel,
        out_shape=outs,
        in_specs=specs,
        out_specs=[VM] * len(outs),
        scratch_shapes=scratch,
        input_output_aliases=dict(aliases),
        compiler_params=params(mebibytes),
        cost_estimate=cost and pl.CostEstimate(flops=cost, bytes_accessed=cost, transcendentals=0),
    )(*args)


def swap(values, axis, odd_pairs):
    devices = lax.axis_size(axis)
    if odd_pairs:
        pairs = [(i, (i + 1) % devices if i % 2 else (i - 1) % devices) for i in range(devices)]
    else:
        pairs = [(i, i ^ 1) for i in range(devices)]
    return lax.ppermute(values, axis, pairs)


def swap_four(t_first, t_second, x_first, x_second):
    xb = swap(x_second, "xyz", True)
    xa = swap(x_first, "xyz", False)
    tb = swap(t_second, "ta", True)
    ta = swap(t_first, "ta", False)
    return ta, tb, xa, xb


def slabs(count, rows):
    return shape((count, rows, LANES), BF16)


def swap_six(ta1, ta2, tb1, tb2, x_first, x_second):
    xb = swap(x_second, "xyz", True)
    xa = swap(x_first, "xyz", False)
    second = [swap(part, "ta", True) for part in (tb1, tb2)]
    return *(swap(part, "ta", False) for part in (ta1, ta2)), *second, xa, xb


def corners_of(fields, deep, *near):
    kernel = functools.partial(corner_kernel, fields, deep)
    *t_parts, xa, xb = near
    beyond = t_parts if deep else ()
    ca, cb = call(kernel, 4, [slabs((2 + 2 * deep) * fields, ROWS)] * 2, [], xb, xa, *beyond)
    cb = swap(cb, "ta", True)
    return swap(ca, "ta", False), cb


def per_device(source, mass, links, near_null, coarse_op, plan):
    out_shape = source.shape
    source = source.reshape(8, LT, ROWS, LANES)
    mass = mass.reshape(LT, ROWS, LANES)
    links = links.reshape(4, LT, ROWS, LANES)
    near_null = near_null.reshape(NVEC, 4, LT, ROWS, LANES)
    coarse_op = coarse_op.reshape(9, NVEC, 2 * NVEC, 32)
    count = 2 * NVEC * RHS
    field, own, ext = (8, LT, ROWS, LANES), (4, LT, 2 * ROWS, LANES), (4, ET, 2 * EROWS, LANES)
    inputs = [shape(ext, F32), shape(ext, F32), shape(ext[1:], F32)]

    plan = pltpu.with_memory_space_constraint(plan, pltpu.HBM)
    source, mass, links, x_a, x_b = call(
        load_kernel,
        8,
        [shape(field, F32), shape(field[1:], F32), shape((4, *field[1:]), I32)] + [slabs(4 * FIELDS + 8, 16)] * 2,
        [pltpu.SemaphoreType.DMA((3,))],
        *(pltpu.with_memory_space_constraint(value, pltpu.HBM) for value in (source, mass, links)),
        far=(0, 1, 2),
    )
    shares = call(share_kernel, 6, [slabs(2 * FIELDS + 4, ROWS)] * 4, [], source, mass, links, cost=1 << 22)
    near = swap_six(*shares, x_a, x_b)
    corners = corners_of(FIELDS, 0, *near)
    coarse_op = pltpu.with_memory_space_constraint(coarse_op, pltpu.HBM)
    *inputs_near, operator = call(
        cross_kernel,
        10,
        inputs + [shape(ext, F32)] * 2 + [shape((7, 6, 2 * NVEC, LANES), F32)],
        [pltpu.VMEM(coarse_op.shape, BF16), pltpu.SMEM((SWEEPS,), I32), pltpu.SemaphoreType.DMA((2,))],
        *near[::-1], source, mass, links, coarse_op, plan,
        far=(9, 10),
        cost=1 << 22,
    )
    solution, rhs, rounded, sent, src, signs, inverse, *_ = call(
        pre_kernel,
        12,
        [shape(field, F32), shape((count, LANES), F32), shape((count, LANES), BF16), shape((32, LANES), BF16)]
        + inputs + [shape(ext, F32)] * 2,
        [(LT, 2 * ROWS, LANES), own, (8 * count, LANES), pltpu.SMEM((SWEEPS,), I32), pltpu.SemaphoreType.DMA],
        plan, mass, *corners, *inputs_near, near_null,
        aliases=((4, 4), (5, 5), (6, 6), (7, 7), (8, 8)),
        far=(0,),
    )
    estimate = rhs
    beside = (7, count, LANES)
    for turn in range(1, KC):
        near = swap_four(sent, sent, sent, sent)
        given = (operator, rhs, estimate, rounded, *near)
        if turn < KC - 1:
            outs = [shape((count, LANES), F32), shape((count, LANES), BF16), shape((32, LANES), BF16)]
            estimate, rounded, sent = call(coarse_kernel, 6, outs, [beside], *given)
    solution, x_a, x_b = call(
        prolong_kernel,
        12,
        [shape(field, F32)] + [slabs(48, 16)] * 2,
        [beside, (count, LANES), (count, 8, LANES)],
        *given, near_null, solution,
    )
    shares = call(share_field_kernel, 4, [slabs(20, ROWS)] * 4, [], solution, cost=1 << 22)
    near = swap_six(*shares, x_a, x_b)
    corners = corners_of(8, 1, *near)
    plan_scratch = [pltpu.SMEM((SWEEPS,), I32), pltpu.SemaphoreType.DMA]
    grown = call(
        field_kernel,
        8,
        [shape(ext, F32)] * 2,
        plan_scratch,
        *near[::-1], solution, src, signs, inverse, plan,
        far=(10,),
        cost=1 << 22,
    )
    solution, residual, *_ = call(
        post_kernel,
        12,
        [shape(field, F32)] * 2 + [shape(ext, F32)] * 2,
        [(LT, 2 * ROWS, LANES), own] + plan_scratch,
        plan, mass, src, signs, inverse, *grown, *corners,
        aliases=((5, 2), (6, 3)),
        far=(0,),
    )
    return solution.reshape(out_shape), residual.reshape(out_shape)


def solution(mesh):
    return jax.shard_map(
        per_device,
        mesh=mesh,
        in_specs=(
            P(None, None, "ta", "xyz", None, None),
            P("ta", "xyz", None, None),
            P(None, "ta", "xyz", None, None),
            P(None, None, "ta", "xyz", None, None),
            P(None, None, None, "ta", "xyz", None, None),
            P(),
        ),
        out_specs=(P(None, None, "ta", "xyz", None, None), P(None, None, "ta", "xyz", None, None)),
        check_vma=False,
    )
```
